32 devices in a mesh: row: 8 (over z, y), proto: 4 (over x, core).
Axes of the slice: x: 2, y: 2, z: 4, core: 2. Of those that a mesh axis runs over, the one named last changes fastest.
Arguments:
- embeddings: bfloat16 [2048, 256], P('row')
- queue_feats: bfloat16 [4096, 256], P('row')
- prototypes: bfloat16 [256, 65536], P('row', 'proto')
- crop_image: int32 [2048], P('row'), may hold values from 0 to 255, as said below
- fill_count: int32 [1], replicated, may hold values from 2048 to 4096
Outputs:
- grad_embed: float32 [2048, 256], P('row')
- grad_proto: float32 [256, 65536], P('row', 'proto')
- loss: float32 [1], replicated
The draws below stay inside these ranges and needn't reach their ends.
Inputs may be any that keep to these rules, and one draw needn't show every extreme that they name: `crop_image`: each image index is named by exactly 8 crops, all within one aligned block of 256 rows (the rows of one device); block b holds images b * 32 to (b + 1) * 32 - 1.
All inputs are finite; a program needn't handle non-finite values.
Results may differ from the reference program's by a relative error of at most 0.002.
Values may be sent and summed in bfloat16 or wider, within the bound.
No kernel may reach another device: no remote copies, remote signals or barrier semaphores. Data moves between devices by JAX's collectives and lax.ppermute only.
A program may use at most 128 MiB of HBM per device.

```python
import math
import jax
import jax.numpy as jnp
from jax import lax

D = 256
PROTOS = 65536
CROPS = 8
ITERS = 3
BATCH_DEV = 256
BATCH = 2048
QUEUE = 4096
IMAGES = 256


def common_direction(key):
    return jax.random.normal(jax.random.fold_in(key, 7), (D,), jnp.float32) / math.sqrt(D)


def banded_loading(key, count, first):
    position = jnp.arange(count, dtype=jnp.float32)
    jitter = jax.random.uniform(jax.random.fold_in(key, first), (count,), jnp.float32, 0.0, 1.0)
    return -1.5 + 3.0 * (position + jitter) / count


def drawn_rows(key, count, first, second):
    direction = common_direction(key)
    along = banded_loading(key, count, first)
    noise = jax.random.normal(jax.random.fold_in(key, second), (count, D), jnp.float32)
    values = along[:, None] * math.sqrt(D) * direction[None, :] + noise
    return values.astype(jnp.bfloat16)


def draw_embeddings(key, part):
    return drawn_rows(key, BATCH, 10, 11)


def draw_queue_feats(key, part):
    return drawn_rows(key, QUEUE, 12, 13)


def draw_prototypes(key, part):
    direction = common_direction(key)
    loading = jax.random.uniform(jax.random.fold_in(key, 8), (PROTOS,), jnp.float32, -0.6, 0.6)
    noise = jax.random.normal(jax.random.fold_in(key, 9), (D, PROTOS), jnp.float32) / math.sqrt(D)
    return (direction[:, None] * loading[None, :] + noise).astype(jnp.bfloat16)


def draw_crop_image(key, part):
    block_total = BATCH // BATCH_DEV
    block_keys = jax.random.split(jax.random.fold_in(key, 21), block_total)
    local_ids = jax.vmap(lambda single: jax.random.permutation(single, BATCH_DEV))(block_keys) // CROPS
    offsets = (jnp.arange(block_total, dtype=jnp.int32) * (BATCH_DEV // CROPS))[:, None]
    return (local_ids.astype(jnp.int32) + offsets).reshape(BATCH).astype(jnp.int32)


def setup_inputs(seed: int = 0) -> dict:
    key_of = jax.random.split(jax.random.key(seed), 6)
    embeddings = draw_embeddings(jax.random.fold_in(key_of[5], 71), 0)
    queue_feats = draw_queue_feats(jax.random.fold_in(key_of[5], 71), 0)
    prototypes = draw_prototypes(jax.random.fold_in(key_of[5], 71), 0)
    crop_image = draw_crop_image(jax.random.fold_in(key_of[5], 71), 0)
    fill_count = jax.random.randint(key_of[4], (1,), QUEUE // 2, QUEUE + 1).astype(jnp.int32)
    return {"embeddings": embeddings, "queue_feats": queue_feats, "prototypes": prototypes, "crop_image": crop_image, "fill_count": fill_count}


ENTROPY_SMOOTHER = 0.05
SOFTMAX_TEMPER = 0.1

def unit_rows(raw):
    values = raw.astype(jnp.float32)
    inverse = lax.rsqrt(lax.optimization_barrier(jnp.sum(values * values, axis=1, keepdims=True)) + 1e-06)
    return (values * inverse, inverse)

def reference(embeddings, queue_feats, prototypes, crop_image, fill_count):
    normed_exact, inverse = unit_rows(embeddings)
    normed = normed_exact.astype(jnp.bfloat16)
    queue_normed = unit_rows(queue_feats)[0].astype(jnp.bfloat16)
    rows_all = jnp.concatenate([normed, queue_normed], axis=0)
    queue_live = (jnp.arange(QUEUE, dtype=jnp.int32) < fill_count[0]).astype(jnp.float32)
    live = jnp.concatenate([jnp.ones((BATCH,), jnp.float32), queue_live])
    block_cols = min(PROTOS, 4096)
    block_count = PROTOS // block_cols
    blocks = prototypes.reshape(D, block_count, block_cols).transpose(1, 0, 2)

    def column_totals(centroid_matrix):

        def column_block(proto_block):
            centroid_similarity = jnp.dot(rows_all, proto_block, preferred_element_type=jnp.float32)
            return lax.optimization_barrier(jnp.sum(jnp.exp(centroid_similarity / ENTROPY_SMOOTHER) * centroid_matrix[:, None], axis=0))
        return lax.map(column_block, blocks).reshape(PROTOS)

    def row_totals(column):

        def row_block(cumulative_accumulator, inputs_pair):
            proto_block, cluster_rescaling = inputs_pair
            centroid_similarity = jnp.dot(rows_all, proto_block, preferred_element_type=jnp.float32)
            return (cumulative_accumulator + lax.optimization_barrier(jnp.sum(jnp.exp(centroid_similarity / ENTROPY_SMOOTHER) * cluster_rescaling[None, :], axis=1)), None)
        row_total, _ = lax.scan(row_block, jnp.zeros((BATCH + QUEUE,), jnp.float32), (blocks, column.reshape(block_count, block_cols)))
        return row_total
    centroid_matrix = live
    column = jnp.zeros((PROTOS,), jnp.float32)
    for sweep_index in range(ITERS):
        column = 1.0 / column_totals(centroid_matrix)
        if sweep_index + 1 < ITERS:
            centroid_matrix = live / row_totals(column)
    column_blocks = column.reshape(block_count, block_cols)

    def totals(cumulative_accumulator, inputs_pair):
        proto_block, cluster_rescaling = inputs_pair
        centroid_similarity = jnp.dot(normed, proto_block, preferred_element_type=jnp.float32)
        allotment_share = lax.optimization_barrier(jnp.sum(jnp.exp(centroid_similarity / ENTROPY_SMOOTHER) * cluster_rescaling[None, :], axis=1))
        softmax_portion = lax.optimization_barrier(jnp.sum(jnp.exp(centroid_similarity / SOFTMAX_TEMPER), axis=1))
        return ((cumulative_accumulator[0] + allotment_share, cumulative_accumulator[1] + softmax_portion), None)
    zeros_batch = jnp.zeros((BATCH,), jnp.float32)
    (overall_mass_sum, softmax_total), _ = lax.scan(totals, (zeros_batch, zeros_batch), (blocks, column_blocks))
    log_grand_total = jnp.log(softmax_total)

    def gradients(cumulative_accumulator, inputs_pair):
        proto_block, cluster_rescaling = inputs_pair
        centroid_similarity = jnp.dot(normed, proto_block, preferred_element_type=jnp.float32)
        cluster_allotment = jnp.exp(centroid_similarity / ENTROPY_SMOOTHER) * cluster_rescaling[None, :] / overall_mass_sum[:, None]
        grouped = jax.ops.segment_sum(cluster_allotment, crop_image, num_segments=IMAGES)
        target_codes = (grouped[crop_image] - cluster_allotment) / (CROPS - 1)
        predicted_probs = jnp.exp(centroid_similarity / SOFTMAX_TEMPER) / softmax_total[:, None]
        logit_gradient = ((predicted_probs - target_codes) / SOFTMAX_TEMPER).astype(jnp.bfloat16)
        loss_portion = jnp.sum(target_codes * (log_grand_total[:, None] - centroid_similarity / SOFTMAX_TEMPER))
        grad_block = lax.dot_general(normed, logit_gradient, (((0,), (0,)), ((), ())), preferred_element_type=jnp.float32)
        normed_part = lax.dot_general(logit_gradient, proto_block, (((1,), (1,)), ((), ())), preferred_element_type=jnp.float32)
        return ((cumulative_accumulator[0] + normed_part, cumulative_accumulator[1] + loss_portion), grad_block)
    (normed_grad, loss_total), grad_blocks = lax.scan(gradients, (jnp.zeros((BATCH, D), jnp.float32), jnp.zeros((), jnp.float32)), (blocks, column_blocks))
    grad_proto = grad_blocks.transpose(1, 0, 2).reshape(D, PROTOS)
    grad_embed = inverse * (normed_grad - normed_exact * lax.optimization_barrier(jnp.sum(normed_exact * normed_grad, axis=1, keepdims=True)))
    loss = (loss_total / BATCH).reshape(1)
    return (grad_embed, grad_proto, loss)
```

```python
import functools

import jax
import jax.numpy as jnp
from jax import lax
from jax.experimental import pallas as pl
from jax.experimental.pallas import tpu as pltpu
from jax.sharding import PartitionSpec as P

CROPS = 8
LOG2E = 1.4426950408889634
SOFT_SCALE = 10.0 * LOG2E
BLOCK = 1024
WIDE = 256

f32 = jnp.float32
bf16 = jnp.bfloat16
f16 = jnp.float16

VMEM = pl.BlockSpec(memory_space=pltpu.VMEM)
SMEM = pl.BlockSpec(memory_space=pltpu.SMEM)
ANY = pl.BlockSpec(memory_space=pl.ANY)


def limit(mib):
    return pltpu.CompilerParams(vmem_limit_bytes=mib << 20)


def bf16_terms(values):
    high = values.astype(bf16)
    rest = values - high.astype(f32)
    middle = rest.astype(bf16)
    return high, middle, (rest - middle.astype(f32)).astype(bf16)


def term_rows(values):
    high, middle, low = bf16_terms(values)
    return jnp.concatenate([high, middle, low] + [jnp.zeros_like(high)] * 5, axis=0)


def sum_terms(products):
    return products[0:1] + products[1:2] + products[2:3]


def dot_nt(left, right):
    return lax.dot_general(left, right, (((1,), (1,)), ((), ())), preferred_element_type=f32)


def dot_tn(left, right):
    return lax.dot_general(left, right, (((0,), (0,)), ((), ())), preferred_element_type=f32)


def unit_rows(raw):
    values = raw.astype(f32)
    inverse = lax.rsqrt(jnp.sum(values * values, axis=1, keepdims=True) + 1e-06)
    return values * inverse, inverse


def prep_kernel(place_ref, image_ref, embed_ref, queue_ref, unit_ref, order_ref, sorted_ref, queued_ref):
    row, core = place_ref[0], place_ref[1]
    rows = embed_ref.shape[0]
    half = rows // 2
    images = half // CROPS
    local = image_ref[...] - row * (rows // CROPS)
    across = jnp.broadcast_to(local, (rows, rows)).astype(f32)
    down = jnp.transpose(across, (1, 0))
    first = lax.broadcasted_iota(jnp.int32, (rows, rows), 0)
    second = lax.broadcasted_iota(jnp.int32, (rows, rows), 1)
    earlier = jnp.where((across == down) & (first < second), 1.0, 0.0)
    rank = jnp.sum(earlier, axis=0, keepdims=True).astype(jnp.int32)
    upper = jnp.where(local >= images, 1, 0)
    position = upper * half + rank * images + (local - upper * images)
    order = (first == position).astype(f32).astype(bf16)
    order_ref[...] = order
    normed = unit_rows(embed_ref[...])[0].astype(bf16)
    sorted_ref[...] = jnp.dot(order, normed, preferred_element_type=f32)
    queued_ref[...] = unit_rows(queue_ref[...])[0]
    queue_half = queue_ref.shape[0] // 2
    unit_ref[0:half, :] = sorted_ref[pl.ds(pl.multiple_of(core * half, half), half), :].astype(bf16)
    unit_ref[half : half + queue_half, :] = queued_ref[
        pl.ds(pl.multiple_of(core * queue_half, queue_half), queue_half), :
    ].astype(bf16)


def row_sums(column, total_batch, queue_blocks, mass_ref, out_ref):
    def one(index, carry):
        start = pl.multiple_of(index * BLOCK, BLOCK)
        out_ref[0:1, pl.ds(start, BLOCK)] = sum_terms(dot_nt(column, mass_ref[pl.ds(start, BLOCK), :]))
        return carry

    lax.fori_loop(0, total_batch // BLOCK + queue_blocks, one, 0)


def live_blocks(fill):
    return lax.div(fill + (BLOCK - 1), BLOCK)


def make_kernel(row_count, half, queue_half, total_batch, place_ref, fill_ref, columns_ref, *refs):
    units = refs[: row_count * 2]
    mass_ref, sums_ref, batch_ref, queue_ref, col_ref, sems = refs[row_count * 2 :]
    row, core = place_ref[0], place_ref[1]
    fill = fill_ref[0]
    copies = []
    for index, unit in enumerate(units):
        place = (row ^ (index // 2)) * 2 + (core ^ (index % 2))
        crops = pl.multiple_of(place * half, half)
        queued = pl.multiple_of(place * queue_half, queue_half)
        copies.append(
            pltpu.make_async_copy(
                unit.at[pl.ds(0, half), :], batch_ref.at[pl.ds(crops, half), :], sems.at[2 * index]
            )
        )
        copies.append(
            pltpu.make_async_copy(
                unit.at[pl.ds(half, queue_half), :],
                queue_ref.at[pl.ds(queued, queue_half), :],
                sems.at[2 * index + 1],
            )
        )
    for copy in copies:
        copy.start()
    total_queue = queue_ref.shape[0]
    total_rows = total_batch + total_queue
    width = columns_ref.shape[1]
    col_ref[...] = jnp.zeros_like(col_ref)
    sums_ref[...] = jnp.zeros_like(sums_ref)
    ones = jnp.ones((8, 128), bf16)
    bound = jnp.max(jnp.abs(columns_ref[...].astype(f32)))
    sums_ref[0:1, total_rows + total_batch : total_rows + total_batch + 128] = jnp.full((1, 128), bound, f32)
    for copy in copies:
        copy.wait()

    def add_columns(low, mass):
        col_ref[:, low : low + WIDE] += jnp.sum(mass.reshape(BLOCK // 8, 8, WIDE), axis=0)

    def crops_block(index, carry):
        start = pl.multiple_of(index * BLOCK, BLOCK)
        rows = batch_ref[pl.ds(start, BLOCK), :]
        lanes = None
        for low in range(0, width, WIDE):
            scores = jnp.dot(rows, columns_ref[:, low : low + WIDE], preferred_element_type=f32)
            soft = jnp.exp2(scores * SOFT_SCALE)
            mass = soft * soft
            mass_ref[pl.ds(start, BLOCK), low : low + WIDE] = mass.astype(bf16)
            add_columns(low, mass)
            for lane in range(0, WIDE, 128):
                part = soft[:, lane : lane + 128]
                lanes = part if lanes is None else lanes + part
        high, middle, small = bf16_terms(lanes)
        total = dot_nt(ones, high) + dot_nt(ones, middle) + dot_nt(ones, small)
        sums_ref[0:1, pl.ds(pl.multiple_of(total_rows + start, BLOCK), BLOCK)] = total[0:1]
        return carry

    lax.fori_loop(0, total_batch // BLOCK, crops_block, 0)

    def queue_block(index, carry):
        start = pl.multiple_of(index * BLOCK, BLOCK)
        rows = queue_ref[pl.ds(start, BLOCK), :]
        live = lax.broadcasted_iota(jnp.int32, (BLOCK, WIDE), 0) < fill - start
        place = pl.ds(pl.multiple_of(total_batch + start, BLOCK), BLOCK)
        for low in range(0, width, WIDE):
            scores = jnp.dot(rows, columns_ref[:, low : low + WIDE], preferred_element_type=f32)
            soft = jnp.exp2(scores * SOFT_SCALE)
            mass = jnp.where(live, soft * soft, 0.0)
            mass_ref[place, low : low + WIDE] = mass.astype(bf16)
            add_columns(low, mass)
        return carry

    lax.fori_loop(0, live_blocks(fill), queue_block, 0)
    column = term_rows(1.0 / jnp.sum(col_ref[...], axis=0, keepdims=True))
    row_sums(column, total_batch, live_blocks(fill), mass_ref, sums_ref)


def column_factor(fill, total_batch, parts, mass_ref, scale_ref, col_ref):
    total_rows = mass_ref.shape[0]
    total = parts[0][0:1, 0:total_rows]
    for part in parts[1:]:
        total = total + part[0:1, 0:total_rows]
    place = lax.broadcasted_iota(jnp.int32, (1, total_rows), 1)
    scale = jnp.where(place < total_batch + fill, 1.0 / total, 0.0)
    scale_ref[...] = term_rows(scale)
    col_ref[...] = jnp.zeros_like(col_ref)

    def one(index, carry):
        rows = pl.ds(pl.multiple_of(index * BLOCK, BLOCK), BLOCK)
        col_ref[...] += jnp.dot(scale_ref[:, rows], mass_ref[rows, :], preferred_element_type=f32)
        return carry

    lax.fori_loop(0, total_batch // BLOCK + live_blocks(fill), one, 0)
    return 1.0 / sum_terms(col_ref[...])


def sweep_kernel(total_batch, fill_ref, mass_ref, *refs):
    *parts, sums_ref, scale_ref, col_ref = refs
    fill = fill_ref[0]
    column = column_factor(fill, total_batch, parts, mass_ref, scale_ref, col_ref)
    sums_ref[...] = jnp.zeros_like(sums_ref)
    row_sums(term_rows(column), total_batch, live_blocks(fill), mass_ref, sums_ref)


def last_kernel(total_batch, fill_ref, mass_ref, *refs):
    *parts, sums_ref, column_ref, scale_ref, col_ref = refs
    fill = fill_ref[0]
    column = column_factor(fill, total_batch, parts, mass_ref, scale_ref, col_ref)
    column_ref[...] = column
    row_sums(term_rows(column), total_batch, 0, mass_ref, sums_ref)


def slope_kernel(crop_count, batch_ref, columns_ref, column_ref, *refs):
    *parts, soft_ref, normed_ref, grad_ref, loss_ref = refs
    total_batch, width = batch_ref.shape[0], columns_ref.shape[1]
    rows = 256
    wide = min(width, 512)
    grad_ref[...] = jnp.zeros_like(grad_ref)
    loss_ref[...] = jnp.zeros_like(loss_ref)

    def one(index, carry):
        start = pl.multiple_of(index * rows, rows)
        here = pl.ds(start, rows)

        def down(line, factor):
            return jnp.transpose(jnp.broadcast_to(factor(line), (128, rows)), (1, 0))[:, 0:1]

        code = parts[0][0:1, here]
        for part in parts[1:]:
            code = code + part[0:1, here]
        code_factor = down(code, lambda line: 1.0 / ((crop_count - 1) * line))
        soft_line = soft_ref[0:1, here]
        soft_factor = down(soft_line, lambda line: 10.0 / line)
        log_soft = down(soft_line, jnp.log)
        crops = batch_ref[here, :]
        crops_t = jnp.transpose(crops.astype(f32), (1, 0)).astype(bf16)
        normed = jnp.zeros((rows, crops.shape[1]), f32)
        loss = jnp.zeros((8, 128), f32)
        for low in range(0, width, wide):
            columns = columns_ref[:, low : low + wide]
            scores = jnp.dot(crops, columns, preferred_element_type=f32)
            soft = jnp.exp2(scores * SOFT_SCALE)
            assigned = (soft * soft) * column_ref[0:1, low : low + wide] * code_factor
            slabs = assigned.reshape(rows // 128, crop_count, 128 // crop_count, wide)
            grouped = jnp.sum(slabs, axis=1, keepdims=True)
            targets = (grouped - slabs).reshape(rows, wide)
            logits = (soft * soft_factor - targets * 10.0).astype(bf16)
            terms = targets * (log_soft - scores * 10.0)
            folded = jnp.sum(terms.reshape(rows // 8, 8, wide), axis=0)
            for lane in range(0, wide, 128):
                loss = loss + folded[:, lane : lane + 128]
            grad_ref[:, low : low + wide] += jnp.dot(crops_t, logits, preferred_element_type=f32)
            normed = normed + dot_nt(logits, columns)
        normed_ref[here, :] = normed
        loss_ref[...] += loss
        return carry

    lax.fori_loop(0, total_batch // rows, one, 0)


def finish_kernel(piece_count, proto_ref, embed_ref, order_ref, *refs):
    pieces, out_ref, sorted_ref = refs[:piece_count], refs[piece_count], refs[piece_count + 1]
    rows = embed_ref.shape[0]
    size = rows // piece_count
    proto = proto_ref[0]
    for index, piece in enumerate(pieces):
        other = proto ^ index
        place = (other % 2) * (piece_count // 2) + other // 2
        sorted_ref[pl.ds(pl.multiple_of(place * size, size), size), :] = piece[...]
    order = order_ref[...]
    high, middle, low = bf16_terms(sorted_ref[...])
    grad = dot_tn(order, high) + dot_tn(order, middle) + dot_tn(order, low)
    exact, inverse = unit_rows(embed_ref[...])
    out_ref[...] = inverse * (grad - exact * jnp.sum(exact * grad, axis=1, keepdims=True))


def solution(mesh):
    row_count, proto_count = mesh.shape["row"], mesh.shape["proto"]
    z_count = min(4, row_count)
    y_count = row_count // z_count
    x_count = proto_count // 2

    def shift_row(values, z, y):
        offset = z * y_count + y
        return lax.ppermute(values, "row", [(i, i ^ offset) for i in range(row_count)])

    def shift_proto(values, offset):
        return lax.ppermute(values, "proto", [(i, i ^ offset) for i in range(proto_count)])

    def shift_xy(values, x, y):
        pairs = []
        for i in range(row_count):
            for j in range(proto_count):
                pairs.append((i * proto_count + j, (i ^ y) * proto_count + (j ^ (2 * x))))
        return lax.ppermute(values, ("row", "proto"), pairs)

    def all_sum_parts(values):
        for offset in range(1, proto_count):
            pass
        moved = [shift_proto(values, offset) for offset in range(1, proto_count)]
        values = functools.reduce(jnp.add, moved, values)
        moved = [shift_row(values, 0, y) for y in range(1, y_count)]
        values = functools.reduce(jnp.add, moved, values)
        return [values] + [shift_row(values, z, 0) for z in range(1, z_count)]

    def body(embeddings, queue_feats, prototypes, crop_image, fill_count):
        batch_rows, feat = embeddings.shape
        queue_rows = queue_feats.shape[0]
        half, queue_half = batch_rows // 2, queue_rows // 2
        total_batch, total_queue = batch_rows * row_count, queue_rows * row_count
        total_rows = total_batch + total_queue
        row, proto = lax.axis_index("row"), lax.axis_index("proto")
        core, x, y, z = proto % 2, proto // 2, row % y_count, row // y_count
        place = jnp.stack([row, core]).astype(jnp.int32)
        unit_rows_count = half + queue_half

        unit, order = pl.pallas_call(
            prep_kernel,
            name="prep",
            out_shape=[
                jax.ShapeDtypeStruct((unit_rows_count, feat), bf16),
                jax.ShapeDtypeStruct((batch_rows, batch_rows), bf16),
            ],
            in_specs=[SMEM, VMEM, VMEM, VMEM],
            out_specs=[VMEM, VMEM],
            scratch_shapes=[pltpu.VMEM((batch_rows, feat), f32), pltpu.VMEM((queue_rows, feat), f32)],
            compiler_params=limit(12),
        )(place, crop_image.reshape(1, batch_rows), embeddings, queue_feats)

        columns = lax.all_to_all(prototypes, "row", split_axis=1, concat_axis=0, tiled=True)
        width = columns.shape[1]

        units = {(0, 0, 0): unit}
        for dz in range(1, z_count):
            units[dz, 0, 0] = shift_row(unit, dz, 0)
        for dy in range(1, y_count):
            for dz in range(z_count):
                units[dz, dy, 0] = shift_row(units[dz, 0, 0], 0, dy)
        for dz in range(z_count):
            for dy in range(y_count):
                units[dz, dy, 1] = shift_proto(units[dz, dy, 0], 1)
        unit_list = [units[i // y_count, i % y_count, c] for i in range(row_count) for c in range(2)]

        sums_size = total_rows + total_batch + 128
        mass, sums, batch = pl.pallas_call(
            functools.partial(make_kernel, row_count, half, queue_half, total_batch),
            name="make_mass",
            out_shape=[
                jax.ShapeDtypeStruct((total_rows, width), bf16),
                jax.ShapeDtypeStruct((1, sums_size), f32),
                jax.ShapeDtypeStruct((total_batch, feat), bf16),
            ],
            in_specs=[SMEM, SMEM, VMEM] + [ANY] * len(unit_list),
            out_specs=[VMEM, VMEM, VMEM],
            scratch_shapes=[
                pltpu.VMEM((total_queue, feat), bf16),
                pltpu.VMEM((8, width), f32),
                pltpu.SemaphoreType.DMA((2 * len(unit_list),)),
            ],
            compiler_params=limit(20),
        )(place, fill_count, columns, *unit_list)

        vectors = [pltpu.VMEM((8, total_rows), bf16), pltpu.VMEM((8, width), f32)]
        first_parts = all_sum_parts(sums)
        sums = pl.pallas_call(
            functools.partial(sweep_kernel, total_batch),
            name="sweep",
            out_shape=jax.ShapeDtypeStruct((1, total_rows), f32),
            in_specs=[SMEM] + [VMEM] * (1 + z_count),
            out_specs=VMEM,
            scratch_shapes=vectors,
            compiler_params=limit(8),
        )(fill_count, mass, *first_parts)
        side = functools.reduce(jnp.add, [part[:, total_rows:] for part in first_parts])
        soft_total, bound = side[:, :total_batch], side[0, total_batch]

        code_sums, column = pl.pallas_call(
            functools.partial(last_kernel, total_batch),
            name="last_sweep",
            out_shape=[
                jax.ShapeDtypeStruct((1, total_batch), f32),
                jax.ShapeDtypeStruct((1, width), f32),
            ],
            in_specs=[SMEM] + [VMEM] * (1 + z_count),
            out_specs=[VMEM, VMEM],
            scratch_shapes=vectors,
            compiler_params=limit(8),
        )(fill_count, mass, *all_sum_parts(sums))

        normed_part, grad_columns, loss = pl.pallas_call(
            functools.partial(slope_kernel, CROPS),
            name="slopes",
            out_shape=[
                jax.ShapeDtypeStruct((total_batch, feat), f32),
                jax.ShapeDtypeStruct((feat, width), f32),
                jax.ShapeDtypeStruct((8, 128), f32),
            ],
            in_specs=[VMEM] * (4 + z_count),
            out_specs=[VMEM] * 3,
            compiler_params=limit(24),
        )(batch, columns, column, *all_sum_parts(code_sums), soft_total)

        grad_parts = lax.all_to_all(grad_columns.astype(f16), "row", split_axis=0, concat_axis=1, tiled=True)
        grad_proto = grad_parts.astype(f32)

        scale = 32768.0 / (20.0 * bound + 1e-30)
        back = 1.0 / scale
        size = half // x_count
        pieces = normed_part.reshape(z_count, y_count, 2, x_count, size, feat)

        def pick(values, index, axis):
            return lax.dynamic_index_in_dim(values, index, axis, keepdims=False)

        away = shift_proto((pick(pieces, 1 - core, 2) * scale).astype(f16), 1)
        kept = pick(pieces, core, 2) + away.astype(f32) * back
        total = None
        for dy in range(y_count):
            for dx in range(x_count):
                part = pick(pick(kept, x ^ dx, 2), y ^ dy, 1)
                if dx or dy:
                    part = shift_xy((part * scale).astype(f16), dx, dy * 1).astype(f32) * back
                total = part if total is None else total + part
        piece = pick(total, z, 0)
        for dz in range(1, z_count):
            moved = shift_row((pick(total, z ^ dz, 0) * scale).astype(f16), dz, 0)
            piece = piece + moved.astype(f32) * back
        gathered = [piece] + [shift_proto(piece, k) for k in range(1, proto_count)]
        grad_embed = pl.pallas_call(
            functools.partial(finish_kernel, proto_count),
            name="finish",
            out_shape=jax.ShapeDtypeStruct((batch_rows, feat), f32),
            in_specs=[SMEM] + [VMEM] * (2 + proto_count),
            out_specs=VMEM,
            scratch_shapes=[pltpu.VMEM((batch_rows, feat), f32)],
            compiler_params=limit(8),
        )(proto.reshape(1).astype(jnp.int32), embeddings, order, *gathered)

        loss_parts = all_sum_parts(jnp.sum(loss).reshape(1))
        loss = functools.reduce(jnp.add, loss_parts) / total_batch
        return grad_embed, grad_proto, loss

    placed = (P("row", None), P("row", None), P("row", "proto"), P("row"), P())
    return jax.shard_map(
        body,
        mesh=mesh,
        in_specs=placed,
        out_specs=(P("row", None), P("row", "proto"), P()),
        check_vma=False,
    )
```

```python
import functools

import jax
import jax.numpy as jnp
from jax import lax
from jax.experimental import pallas as pl
from jax.experimental.pallas import tpu as pltpu
from jax.sharding import PartitionSpec as P

CROPS = 8
LOG2E = 1.4426950408889634
SOFT_SCALE = 10.0 * LOG2E
BLOCK = 1024
WIDE = 256
ROWS = 1024

f32 = jnp.float32
bf16 = jnp.bfloat16
f16 = jnp.float16

VMEM = pl.BlockSpec(memory_space=pltpu.VMEM)
SMEM = pl.BlockSpec(memory_space=pltpu.SMEM)
ANY = pl.BlockSpec(memory_space=pl.ANY)


def limit(mib):
    return pltpu.CompilerParams(vmem_limit_bytes=mib << 20)


def bf16_terms(values):
    high = values.astype(bf16)
    rest = values - high.astype(f32)
    middle = rest.astype(bf16)
    return high, middle, (rest - middle.astype(f32)).astype(bf16)


def term_rows(values):
    high, middle, low = bf16_terms(values)
    return jnp.concatenate([high, middle, low] + [jnp.zeros_like(high)] * 5, axis=0)


def sum_terms(products):
    return products[0:1] + products[1:2] + products[2:3]


def dot_nt(left, right):
    return lax.dot_general(left, right, (((1,), (1,)), ((), ())), preferred_element_type=f32)


def dot_tn(left, right):
    return lax.dot_general(left, right, (((0,), (0,)), ((), ())), preferred_element_type=f32)


def unit_rows(raw):
    values = raw.astype(f32)
    inverse = lax.rsqrt(jnp.sum(values * values, axis=1, keepdims=True) + 1e-06)
    return values * inverse, inverse


def prep_kernel(
    place_ref, image_ref, embed_in, queue_in, unit_ref, order_ref, embed_ref, queue_ref, sorted_ref, queued_ref, sems
):
    fetch = [
        pltpu.make_async_copy(embed_in, embed_ref, sems.at[0]),
        pltpu.make_async_copy(queue_in, queue_ref, sems.at[1]),
    ]
    for copy in fetch:
        copy.start()
    row, proto = place_ref[0], place_ref[1]
    rows = embed_ref.shape[0]
    half = rows // 2
    images = half // CROPS
    local = image_ref[...] - row * (rows // CROPS)
    across = jnp.broadcast_to(local, (rows, rows)).astype(f32)
    down = jnp.transpose(across, (1, 0))
    first = lax.broadcasted_iota(jnp.int32, (rows, rows), 0)
    second = lax.broadcasted_iota(jnp.int32, (rows, rows), 1)
    earlier = jnp.where((across == down) & (first < second), 1.0, 0.0)
    rank = jnp.sum(earlier, axis=0, keepdims=True).astype(jnp.int32)
    upper = jnp.where(local >= images, 1, 0)
    position = upper * half + rank * images + (local - upper * images)
    order = (first == position).astype(f32).astype(bf16)
    order_ref[...] = order
    for copy in fetch:
        copy.wait()
    normed = unit_rows(embed_ref[...])[0].astype(bf16)
    sorted_ref[...] = jnp.dot(order, normed, preferred_element_type=f32)
    queued_ref[...] = unit_rows(queue_ref[...])[0]
    share = rows * unit_ref.shape[0] // (rows + queue_ref.shape[0])
    queue_share = unit_ref.shape[0] - share
    unit_ref[0:share, :] = sorted_ref[pl.ds(pl.multiple_of(proto * share, share), share), :].astype(bf16)
    unit_ref[share:, :] = queued_ref[
        pl.ds(pl.multiple_of(proto * queue_share, queue_share), queue_share), :
    ].astype(bf16)


def row_sums(column, total_batch, queue_blocks, mass_ref, out_ref):
    def one(index, carry):
        start = pl.multiple_of(index * BLOCK, BLOCK)
        out_ref[0:1, pl.ds(start, BLOCK)] = sum_terms(dot_nt(column, mass_ref[pl.ds(start, BLOCK), :]))
        return carry

    lax.fori_loop(0, total_batch // BLOCK + queue_blocks, one, 0)


def live_blocks(fill):
    return lax.div(fill + (BLOCK - 1), BLOCK)


def make_kernel(offsets, share, total_batch, place_ref, fill_ref, columns_ref, *refs):
    units = refs[: len(offsets)]
    mass_out, sums_ref, side_ref, batch_ref, mass_ref, queue_ref, col_ref, sems, out_sems = refs[len(offsets) :]
    row, proto = place_ref[0], place_ref[1]
    fill = fill_ref[0]
    z_count, unit_rows_count, _ = units[0].shape
    queue_share = unit_rows_count - share
    proto_count = 1 + max(other for _, other in offsets)
    y_count = 1 + max(y for y, _ in offsets)
    copies = []
    for index, (unit, (y, other)) in enumerate(zip(units, offsets)):
        for z in range(z_count):
            place = (row ^ (z * y_count + y)) * proto_count + (proto ^ other)
            crops = pl.multiple_of(place * share, share)
            queued = pl.multiple_of(place * queue_share, queue_share)
            copies.append(
                pltpu.make_async_copy(
                    unit.at[z, pl.ds(0, share), :],
                    batch_ref.at[pl.ds(crops, share), :],
                    sems.at[index, z, 0],
                )
            )
            copies.append(
                pltpu.make_async_copy(
                    unit.at[z, pl.ds(share, queue_share), :],
                    queue_ref.at[pl.ds(queued, queue_share), :],
                    sems.at[index, z, 1],
                )
            )
    for copy in copies[0::2] + copies[1::2]:
        copy.start()
    total_queue = queue_ref.shape[0]
    width = columns_ref.shape[1]
    col_ref[...] = jnp.zeros_like(col_ref)
    sums_ref[...] = jnp.zeros_like(sums_ref)
    ones = jnp.ones((8, 128), bf16)
    bound = jnp.max(jnp.abs(columns_ref[...].astype(f32)))
    side_ref[0:1, total_batch:] = jnp.full((1, 128), bound, f32)
    for copy in copies[0::2]:
        copy.wait()

    def add_columns(low, mass):
        col_ref[:, low : low + WIDE] += jnp.sum(mass.reshape(BLOCK // 8, 8, WIDE), axis=0)

    def keep(start):
        place = pl.ds(pl.multiple_of(start, BLOCK), BLOCK)
        return pltpu.make_async_copy(mass_ref.at[place, :], mass_out.at[place, :], out_sems)

    def crops_block(index, carry):
        start = pl.multiple_of(index * BLOCK, BLOCK)
        rows = batch_ref[pl.ds(start, BLOCK), :]
        lanes = None
        for low in range(0, width, WIDE):
            scores = jnp.dot(rows, columns_ref[:, low : low + WIDE], preferred_element_type=f32)
            soft = jnp.exp2(scores * SOFT_SCALE)
            mass = soft * soft
            mass_ref[pl.ds(start, BLOCK), low : low + WIDE] = mass.astype(bf16)
            add_columns(low, mass)
            for lane in range(0, WIDE, 128):
                part = soft[:, lane : lane + 128]
                lanes = part if lanes is None else lanes + part
        high, middle, small = bf16_terms(lanes)
        total = dot_nt(ones, high) + dot_nt(ones, middle) + dot_nt(ones, small)
        side_ref[0:1, pl.ds(start, BLOCK)] = total[0:1]
        keep(start).start()
        return carry

    lax.fori_loop(0, total_batch // BLOCK, crops_block, 0)

    for copy in copies[1::2]:
        copy.wait()

    def queue_block(index, carry):
        start = pl.multiple_of(index * BLOCK, BLOCK)
        rows = queue_ref[pl.ds(start, BLOCK), :]
        live = lax.broadcasted_iota(jnp.int32, (BLOCK, WIDE), 0) < fill - start
        place = pl.ds(pl.multiple_of(total_batch + start, BLOCK), BLOCK)
        for low in range(0, width, WIDE):
            scores = jnp.dot(rows, columns_ref[:, low : low + WIDE], preferred_element_type=f32)
            soft = jnp.exp2(scores * SOFT_SCALE)
            mass = jnp.where(live, soft * soft, 0.0)
            mass_ref[place, low : low + WIDE] = mass.astype(bf16)
            add_columns(low, mass)
        keep(total_batch + start).start()
        return carry

    lax.fori_loop(0, live_blocks(fill), queue_block, 0)
    column = term_rows(1.0 / jnp.sum(col_ref[...], axis=0, keepdims=True))
    row_sums(column, total_batch, live_blocks(fill), mass_ref, sums_ref)

    def finish(index, carry):
        keep(index * BLOCK).wait()
        return carry

    lax.fori_loop(0, total_batch // BLOCK + live_blocks(fill), finish, 0)


def column_factor(fill, total_batch, parts, mass_ref, scale_ref, col_ref, ready=None):
    total_rows = mass_ref.shape[0]
    total = parts[0][0:1, 0:total_rows]
    for part in parts[1:]:
        total = total + part[0:1, 0:total_rows]
    place = lax.broadcasted_iota(jnp.int32, (1, total_rows), 1)
    scale = jnp.where(place < total_batch + fill, 1.0 / total, 0.0)
    scale_ref[...] = term_rows(scale)
    col_ref[...] = jnp.zeros_like(col_ref)

    def one(index, carry):
        if ready is not None:
            ready(index)
        rows = pl.ds(pl.multiple_of(index * BLOCK, BLOCK), BLOCK)
        col_ref[...] += jnp.dot(scale_ref[:, rows], mass_ref[rows, :], preferred_element_type=f32)
        return carry

    lax.fori_loop(0, total_batch // BLOCK + live_blocks(fill), one, 0)
    return 1.0 / sum_terms(col_ref[...])


def sweep_kernel(total_batch, fill_ref, mass_in, *refs):
    *parts, sums_ref, mass_ref, scale_ref, col_ref, sems = refs
    fill = fill_ref[0]
    blocks = total_batch // BLOCK + live_blocks(fill)

    def fetch(index):
        rows = pl.ds(pl.multiple_of(index * BLOCK, BLOCK), BLOCK)
        return pltpu.make_async_copy(mass_in.at[rows, :], mass_ref.at[rows, :], sems.at[index])

    def start(index, carry):
        fetch(index).start()
        return carry

    lax.fori_loop(0, blocks, start, 0)
    column = column_factor(
        fill, total_batch, parts, mass_ref, scale_ref, col_ref, lambda index: fetch(index).wait()
    )
    sums_ref[...] = jnp.zeros_like(sums_ref)
    row_sums(term_rows(column), total_batch, live_blocks(fill), mass_ref, sums_ref)


def last_kernel(total_batch, fill_ref, side_ref, mass_ref, *refs):
    *parts, sums_ref, column_ref, scale_ref, col_ref = refs
    fill = fill_ref[0]
    column = column_factor(fill, total_batch, parts, mass_ref, scale_ref, col_ref)
    column_ref[...] = column
    sums_ref[0:1, total_batch:] = side_ref[...]
    row_sums(term_rows(column), total_batch, 0, mass_ref, sums_ref)


def slope_kernel(crop_count, first, last, batch_ref, columns_ref, column_ref, *refs):
    *parts, normed_out, grad_ref, loss_ref, back_ref, normed_ref, sems = refs
    total_batch, width = batch_ref.shape[0], last - first
    rows = ROWS
    wide = min(width, WIDE)
    grad_ref[...] = jnp.zeros_like(grad_ref)
    loss_ref[...] = jnp.zeros_like(loss_ref)

    bound = functools.reduce(jnp.add, [part[0:1, 2 * total_batch :] for part in parts])
    bound = 20.0 * bound + 1e-30
    back_ref[...] = jnp.broadcast_to(bound / 32768.0, (8, 128))
    scale = jnp.concatenate([32768.0 / bound] * (batch_ref.shape[1] // 128), axis=1)

    def keep(index):
        place = pl.ds(pl.multiple_of(index * rows, rows), rows)
        return pltpu.make_async_copy(normed_ref.at[place, :], normed_out.at[place, :], sems.at[index])

    def one(index, carry):
        start = pl.multiple_of(index * rows, rows)
        here = pl.ds(start, rows)

        later = pl.ds(pl.multiple_of(total_batch + start, rows), rows)
        code, soft_line = parts[0][0:1, here], parts[0][0:1, later]
        for part in parts[1:]:
            code, soft_line = code + part[0:1, here], soft_line + part[0:1, later]
        lines = [1.0 / ((crop_count - 1) * code), 10.0 / soft_line, jnp.log(soft_line)]
        factors = jnp.transpose(jnp.concatenate(lines + [jnp.zeros((125, rows), f32)], axis=0), (1, 0))
        code_factor, soft_factor, log_soft = (factors[:, i : i + 1] for i in range(3))
        crops = batch_ref[here, :]
        crops_t = jnp.transpose(crops.astype(f32), (1, 0)).astype(bf16)
        normed = jnp.zeros((rows, crops.shape[1]), f32)
        loss = jnp.zeros((8, 128), f32)
        for low in range(0, width, wide):
            place = slice(first + low, first + low + wide)
            columns = columns_ref[:, place]
            scores = jnp.dot(crops, columns, preferred_element_type=f32)
            soft = jnp.exp2(scores * SOFT_SCALE)
            assigned = (soft * soft) * column_ref[0:1, place] * code_factor
            slabs = assigned.reshape(rows // 128, crop_count, 128 // crop_count, wide)
            grouped = jnp.sum(slabs, axis=1, keepdims=True)
            targets = (grouped - slabs).reshape(rows, wide)
            logits = (soft * soft_factor - targets * 10.0).astype(bf16)
            terms = targets * (log_soft - scores * 10.0)
            folded = jnp.sum(terms.reshape(rows // 8, 8, wide), axis=0)
            for lane in range(0, wide, 128):
                loss = loss + folded[:, lane : lane + 128]
            grad_ref[:, low : low + wide] += jnp.dot(crops_t, logits, preferred_element_type=f32)
            normed = normed + dot_nt(logits, columns)
        normed_ref[here, :] = normed * scale
        keep(index).start()
        loss_ref[...] += loss
        return carry

    lax.fori_loop(0, total_batch // rows, one, 0)

    def kept(index, carry):
        keep(index).wait()
        return carry

    lax.fori_loop(0, total_batch // rows, kept, 0)


def finish_kernel(piece_count, total_batch, proto_ref, embed_ref, order_ref, back_ref, *refs):
    *parts, out_ref, loss_ref, sorted_ref = refs
    pieces, losses = parts[:piece_count], parts[piece_count:]
    rows = embed_ref.shape[0]
    size = rows // piece_count
    proto = proto_ref[0]
    for index, piece in enumerate(pieces):
        other = proto ^ index
        place = (other % 2) * (piece_count // 2) + other // 2
        sorted_ref[pl.ds(pl.multiple_of(place * size, size), size), :] = piece[...]
    loss_ref[0] = jnp.sum(functools.reduce(jnp.add, [loss[...] for loss in losses])) / total_batch
    order = order_ref[...]
    high, middle, low = bf16_terms(sorted_ref[...])
    grad = dot_tn(order, high) + dot_tn(order, middle) + dot_tn(order, low)
    grad = grad * back_ref[0:1, 0:1]
    exact, inverse = unit_rows(embed_ref[...])
    out_ref[...] = inverse * (grad - exact * jnp.sum(exact * grad, axis=1, keepdims=True))


def solution(mesh):
    row_count, proto_count = mesh.shape["row"], mesh.shape["proto"]
    z_count = min(4, row_count)
    y_count = row_count // z_count
    x_count = proto_count // 2

    def shift_row(values, z, y):
        offset = z * y_count + y
        return lax.ppermute(values, "row", [(i, i ^ offset) for i in range(row_count)])

    def shift_proto(values, offset):
        return lax.ppermute(values, "proto", [(i, i ^ offset) for i in range(proto_count)])

    def shift_xy(values, x, y):
        pairs = []
        for i in range(row_count):
            for j in range(proto_count):
                pairs.append((i * proto_count + j, (i ^ y) * proto_count + (j ^ (2 * x))))
        return lax.ppermute(values, ("row", "proto"), pairs)

    def all_sum_parts(values):
        values = values + shift_proto(values, 1)
        moved = [shift_xy(values, x, y) for y in range(y_count) for x in range(x_count) if x or y]
        values = functools.reduce(jnp.add, moved, values)
        return [values] + [shift_row(values, z, 0) for z in range(1, z_count)]

    def body(embeddings, queue_feats, prototypes, crop_image, fill_count):
        batch_rows, feat = embeddings.shape
        queue_rows = queue_feats.shape[0]
        share, queue_share = batch_rows // proto_count, queue_rows // proto_count
        half = batch_rows // 2
        total_batch, total_queue = batch_rows * row_count, queue_rows * row_count
        total_rows = total_batch + total_queue
        row, proto = lax.axis_index("row"), lax.axis_index("proto")
        core, x, y, z = proto % 2, proto // 2, row % y_count, row // y_count
        place = jnp.stack([row, proto]).astype(jnp.int32)
        unit_rows_count = share + queue_share

        unit, order = pl.pallas_call(
            prep_kernel,
            name="prep",
            out_shape=[
                jax.ShapeDtypeStruct((unit_rows_count, feat), bf16),
                jax.ShapeDtypeStruct((batch_rows, batch_rows), bf16),
            ],
            in_specs=[SMEM, VMEM, ANY, ANY],
            out_specs=[VMEM, VMEM],
            scratch_shapes=[
                pltpu.VMEM((batch_rows, feat), bf16),
                pltpu.VMEM((queue_rows, feat), bf16),
                pltpu.VMEM((batch_rows, feat), f32),
                pltpu.VMEM((queue_rows, feat), f32),
                pltpu.SemaphoreType.DMA((2,)),
            ],
            compiler_params=limit(56),
        )(place, crop_image.reshape(1, batch_rows), embeddings, queue_feats)

        lines = jnp.stack([unit] + [shift_row(unit, z, 0) for z in range(1, z_count)])
        width = prototypes.shape[1] // row_count
        blocks = prototypes.reshape(-1, row_count, width).transpose(1, 0, 2)
        lines, blocks = lax.optimization_barrier((lines, blocks))
        columns = lax.all_to_all(blocks, "row", split_axis=0, concat_axis=0, tiled=True).reshape(feat, width)

        offsets, units = [], []
        for dy in range(y_count):
            there = shift_row(lines, 0, dy) if dy else lines
            for dx in range(x_count):
                moved = shift_proto(there, 2 * dx) if dx else there
                offsets += [(dy, 2 * dx), (dy, 2 * dx + 1)]
                units += [moved, shift_proto(moved, 1)]

        mass, sums, side, batch = pl.pallas_call(
            functools.partial(make_kernel, offsets, share, total_batch),
            name="make_mass",
            out_shape=[
                jax.ShapeDtypeStruct((total_rows, width), bf16),
                jax.ShapeDtypeStruct((1, total_rows), f32),
                jax.ShapeDtypeStruct((1, total_batch + 128), f32),
                jax.ShapeDtypeStruct((total_batch, feat), bf16),
            ],
            in_specs=[SMEM, SMEM, VMEM] + [ANY] * len(units),
            out_specs=[ANY, VMEM, VMEM, VMEM],
            scratch_shapes=[
                pltpu.VMEM((total_rows, width), bf16),
                pltpu.VMEM((total_queue, feat), bf16),
                pltpu.VMEM((8, width), f32),
                pltpu.SemaphoreType.DMA((len(units), z_count, 2)),
                pltpu.SemaphoreType.DMA,
            ],
            compiler_params=limit(56),
        )(place, fill_count, columns, *units)

        vectors = [pltpu.VMEM((8, total_rows), bf16), pltpu.VMEM((8, width), f32)]
        sums = pl.pallas_call(
            functools.partial(sweep_kernel, total_batch),
            name="sweep",
            out_shape=jax.ShapeDtypeStruct((1, total_rows), f32),
            in_specs=[SMEM, ANY] + [VMEM] * z_count,
            out_specs=VMEM,
            scratch_shapes=[pltpu.VMEM((total_rows, width), bf16)]
            + vectors
            + [pltpu.SemaphoreType.DMA((total_rows // BLOCK,))],
            compiler_params=limit(30),
        )(fill_count, mass, *all_sum_parts(sums))

        code_sums, column = pl.pallas_call(
            functools.partial(last_kernel, total_batch),
            name="last_sweep",
            out_shape=[
                jax.ShapeDtypeStruct((1, 2 * total_batch + 128), f32),
                jax.ShapeDtypeStruct((1, width), f32),
            ],
            in_specs=[SMEM] + [VMEM] * (2 + z_count),
            out_specs=[VMEM, VMEM],
            scratch_shapes=vectors,
            compiler_params=limit(8),
        )(fill_count, side, mass, *all_sum_parts(sums))

        code_parts = all_sum_parts(code_sums)

        def slopes(first, last, batch):
            return pl.pallas_call(
                functools.partial(slope_kernel, CROPS, first, last),
                name="slopes",
                out_shape=[
                    jax.ShapeDtypeStruct((total_batch, feat), f32),
                    jax.ShapeDtypeStruct((feat, last - first), f32),
                    jax.ShapeDtypeStruct((8, 128), f32),
                    jax.ShapeDtypeStruct((8, 128), f32),
                ],
                in_specs=[VMEM] * (3 + z_count),
                out_specs=[ANY, VMEM, VMEM, VMEM],
                scratch_shapes=[
                    pltpu.VMEM((total_batch, feat), f32),
                    pltpu.SemaphoreType.DMA((total_batch // ROWS,)),
                ],
                compiler_params=limit(24),
            )(batch, columns, column, *code_parts)

        def as_blocks(grad_columns):
            return grad_columns.astype(f16).reshape(row_count, feat // row_count, -1)

        def exchange(blocks):
            return lax.all_to_all(blocks, "row", split_axis=0, concat_axis=0, tiled=True)

        normed_part, grad_columns, loss, back = slopes(0, width, batch)
        size = half // x_count

        def pick(values, index, axis):
            return lax.dynamic_index_in_dim(values, index, axis, keepdims=False)

        pieces = normed_part.reshape(z_count, y_count, 2, x_count, size, feat)

        away = shift_proto(pick(pieces, 1 - core, 2).astype(f16), 1)
        loss = loss + shift_proto(loss, 1)
        kept = pick(pieces, core, 2) + away.astype(f32)
        total, losses = None, None
        for dy in range(y_count):
            for dx in range(x_count):
                part, other = pick(pick(kept, x ^ dx, 2), y ^ dy, 1), loss
                if dx or dy:
                    part = shift_xy(part.astype(f16), dx, dy).astype(f32)
                    other = shift_xy(loss, dx, dy)
                total = part if total is None else total + part
                losses = other if losses is None else losses + other
        piece = pick(total, z, 0)
        loss_parts = [losses]
        for dz in range(1, z_count):
            piece = piece + shift_row(pick(total, z ^ dz, 0).astype(f16), dz, 0).astype(f32)
            loss_parts.append(shift_row(losses, dz, 0))
        piece, *loss_parts = lax.optimization_barrier((piece, *loss_parts))
        grad_proto = exchange(as_blocks(grad_columns)).astype(f32)
        grad_proto = grad_proto.transpose(1, 0, 2).reshape(feat // row_count, row_count * width)

        gathered = [piece] + [shift_proto(piece, k) for k in range(1, proto_count)]
        grad_embed, loss = pl.pallas_call(
            functools.partial(finish_kernel, proto_count, total_batch),
            name="finish",
            out_shape=[
                jax.ShapeDtypeStruct((batch_rows, feat), f32),
                jax.ShapeDtypeStruct((1,), f32),
            ],
            in_specs=[SMEM] + [VMEM] * (3 + proto_count + z_count),
            out_specs=[VMEM, SMEM],
            scratch_shapes=[pltpu.VMEM((batch_rows, feat), f32)],
            compiler_params=limit(8),
        )(proto.reshape(1).astype(jnp.int32), embeddings, order, back, *gathered, *loss_parts)
        return grad_embed, grad_proto, loss

    placed = (P("row", None), P("row", None), P("row", "proto"), P("row"), P())
    return jax.shard_map(
        body,
        mesh=mesh,
        in_specs=placed,
        out_specs=(P("row", None), P("row", "proto"), P()),
        check_vma=False,
    )
```

```python
import functools

import jax
import jax.numpy as jnp
from jax import lax
from jax.experimental import pallas as pl
from jax.experimental.pallas import tpu as pltpu
from jax.sharding import PartitionSpec as P

CROPS = 8
LOG2E = 1.4426950408889634
SOFT_SCALE = 10.0 * LOG2E
BLOCK = 1024
WIDE = 256
ROWS = 1024

f32 = jnp.float32
bf16 = jnp.bfloat16
f16 = jnp.float16

VMEM = pl.BlockSpec(memory_space=pltpu.VMEM)
SMEM = pl.BlockSpec(memory_space=pltpu.SMEM)
ANY = pl.BlockSpec(memory_space=pl.ANY)


def limit(mib):
    return pltpu.CompilerParams(vmem_limit_bytes=mib << 20)


def bf16_terms(values):
    high = values.astype(bf16)
    rest = values - high.astype(f32)
    middle = rest.astype(bf16)
    return high, middle, (rest - middle.astype(f32)).astype(bf16)


def term_rows(values):
    high, middle, low = bf16_terms(values)
    return jnp.concatenate([high, middle, low] + [jnp.zeros_like(high)] * 5, axis=0)


def sum_terms(products):
    return products[0:1] + products[1:2] + products[2:3]


def dot_nt(left, right):
    return lax.dot_general(left, right, (((1,), (1,)), ((), ())), preferred_element_type=f32)


def dot_tn(left, right):
    return lax.dot_general(left, right, (((0,), (0,)), ((), ())), preferred_element_type=f32)


def unit_rows(raw):
    values = raw.astype(f32)
    inverse = lax.rsqrt(jnp.sum(values * values, axis=1, keepdims=True) + 1e-06)
    return values * inverse, inverse


def prep_kernel(
    place_ref, image_ref, embed_in, queue_in, unit_ref, order_ref, embed_ref, queue_ref, sorted_ref, queued_ref, sems
):
    fetch = [
        pltpu.make_async_copy(embed_in, embed_ref, sems.at[0]),
        pltpu.make_async_copy(queue_in, queue_ref, sems.at[1]),
    ]
    for copy in fetch:
        copy.start()
    row, proto = place_ref[0], place_ref[1]
    rows = embed_ref.shape[0]
    half = rows // 2
    images = half // CROPS
    local = image_ref[...] - row * (rows // CROPS)
    across = jnp.broadcast_to(local, (rows, rows)).astype(f32)
    down = jnp.transpose(across, (1, 0))
    first = lax.broadcasted_iota(jnp.int32, (rows, rows), 0)
    second = lax.broadcasted_iota(jnp.int32, (rows, rows), 1)
    earlier = jnp.where((across == down) & (first < second), 1.0, 0.0)
    rank = jnp.sum(earlier, axis=0, keepdims=True).astype(jnp.int32)
    upper = jnp.where(local >= images, 1, 0)
    position = upper * half + rank * images + (local - upper * images)
    order = (first == position).astype(f32).astype(bf16)
    order_ref[...] = order
    for copy in fetch:
        copy.wait()
    normed = unit_rows(embed_ref[...])[0].astype(bf16)
    sorted_ref[...] = jnp.dot(order, normed, preferred_element_type=f32)
    queued_ref[...] = unit_rows(queue_ref[...])[0]
    share = rows * unit_ref.shape[0] // (rows + queue_ref.shape[0])
    queue_share = unit_ref.shape[0] - share
    unit_ref[0:share, :] = sorted_ref[pl.ds(pl.multiple_of(proto * share, share), share), :].astype(bf16)
    unit_ref[share:, :] = queued_ref[
        pl.ds(pl.multiple_of(proto * queue_share, queue_share), queue_share), :
    ].astype(bf16)


def row_sums(column, total_batch, queue_blocks, mass_ref, out_ref, wide=None):
    head = wide or BLOCK // 4
    width = mass_ref.shape[1]
    step = 128
    factor = column[0:1]
    ones = jnp.ones((8, 128), bf16)

    def one(index, carry):
        start = pl.multiple_of(index * BLOCK, BLOCK)
        out_ref[0:1, pl.ds(start, head)] = sum_terms(dot_nt(column, mass_ref[pl.ds(start, head), :]))
        for rows in range(head, BLOCK, step):
            here = pl.ds(pl.multiple_of(start + rows, step), step)
            total = None
            for low in range(0, width, 256):
                pair = mass_ref[here, low : low + 128] * factor[:, low : low + 128]
                pair += mass_ref[here, low + 128 : low + 256] * factor[:, low + 128 : low + 256]
                total = pair.astype(f32) if total is None else total + pair.astype(f32)
            high = total.astype(bf16)
            low = (total - high.astype(f32)).astype(bf16)
            out_ref[0:1, here] = (dot_nt(ones, high) + dot_nt(ones, low))[0:1]
        return carry

    lax.fori_loop(0, total_batch // BLOCK + queue_blocks, one, 0)


def live_blocks(fill):
    return lax.div(fill + (BLOCK - 1), BLOCK)


def make_kernel(offsets, share, total_batch, place_ref, fill_ref, columns_ref, *refs):
    units = refs[: len(offsets)]
    mass_out, sums_ref, side_ref, batch_ref, mass_ref, queue_ref, col_ref, sems, out_sems = refs[len(offsets) :]
    row, proto = place_ref[0], place_ref[1]
    fill = fill_ref[0]
    z_count, unit_rows_count, _ = units[0].shape
    queue_share = unit_rows_count - share
    proto_count = 1 + max(other for _, other in offsets)
    y_count = 1 + max(y for y, _ in offsets)
    copies = []
    for index, (unit, (y, other)) in enumerate(zip(units, offsets)):
        for z in range(z_count):
            place = (row ^ (z * y_count + y)) * proto_count + (proto ^ other)
            crops = pl.multiple_of(place * share, share)
            queued = pl.multiple_of(place * queue_share, queue_share)
            copies.append(
                pltpu.make_async_copy(
                    unit.at[z, pl.ds(0, share), :],
                    batch_ref.at[pl.ds(crops, share), :],
                    sems.at[index, z, 0],
                )
            )
            copies.append(
                pltpu.make_async_copy(
                    unit.at[z, pl.ds(share, queue_share), :],
                    queue_ref.at[pl.ds(queued, queue_share), :],
                    sems.at[index, z, 1],
                )
            )
    for copy in copies[0::2] + copies[1::2]:
        copy.start()
    total_queue = queue_ref.shape[0]
    width = columns_ref.shape[1]
    col_ref[...] = jnp.zeros_like(col_ref)
    sums_ref[...] = jnp.zeros_like(sums_ref)
    ones = jnp.ones((8, 128), bf16)
    bound = jnp.max(jnp.abs(columns_ref[...].astype(f32)))
    side_ref[0:1, total_batch:] = jnp.full((1, 128), bound, f32)
    for copy in copies[0::2]:
        copy.wait()

    def add_columns(low, mass):
        col_ref[:, low : low + WIDE] += jnp.sum(mass.reshape(BLOCK // 8, 8, WIDE), axis=0)

    def keep(start):
        place = pl.ds(pl.multiple_of(start, BLOCK), BLOCK)
        return pltpu.make_async_copy(mass_ref.at[place, :], mass_out.at[place, :], out_sems)

    def crops_block(index, carry):
        start = pl.multiple_of(index * BLOCK, BLOCK)
        rows = batch_ref[pl.ds(start, BLOCK), :]
        lanes = None
        for low in range(0, width, WIDE):
            scores = jnp.dot(rows, columns_ref[:, low : low + WIDE], preferred_element_type=f32)
            soft = jnp.exp2(scores * SOFT_SCALE)
            mass = soft * soft
            mass_ref[pl.ds(start, BLOCK), low : low + WIDE] = mass.astype(bf16)
            add_columns(low, mass)
            for lane in range(0, WIDE, 128):
                part = soft[:, lane : lane + 128]
                lanes = part if lanes is None else lanes + part
        high, middle, small = bf16_terms(lanes)
        total = dot_nt(ones, high) + dot_nt(ones, middle) + dot_nt(ones, small)
        side_ref[0:1, pl.ds(start, BLOCK)] = total[0:1]
        keep(start).start()
        return carry

    lax.fori_loop(0, total_batch // BLOCK, crops_block, 0)

    for copy in copies[1::2]:
        copy.wait()

    def queue_block(index, carry):
        start = pl.multiple_of(index * BLOCK, BLOCK)
        rows = queue_ref[pl.ds(start, BLOCK), :]
        live = lax.broadcasted_iota(jnp.int32, (BLOCK, WIDE), 0) < fill - start
        place = pl.ds(pl.multiple_of(total_batch + start, BLOCK), BLOCK)
        for low in range(0, width, WIDE):
            scores = jnp.dot(rows, columns_ref[:, low : low + WIDE], preferred_element_type=f32)
            soft = jnp.exp2(scores * SOFT_SCALE)
            mass = jnp.where(live, soft * soft, 0.0)
            mass_ref[place, low : low + WIDE] = mass.astype(bf16)
            add_columns(low, mass)
        keep(total_batch + start).start()
        return carry

    lax.fori_loop(0, live_blocks(fill), queue_block, 0)
    column = term_rows(1.0 / jnp.sum(col_ref[...], axis=0, keepdims=True))
    row_sums(column, total_batch, live_blocks(fill), mass_ref, sums_ref)

    def finish(index, carry):
        keep(index * BLOCK).wait()
        return carry

    lax.fori_loop(0, total_batch // BLOCK + live_blocks(fill), finish, 0)


def column_factor(fill, total_batch, parts, mass_ref, scale_ref, col_ref, spare_ref, make=None, ready=None):
    total_rows = mass_ref.shape[0]
    total = parts[0][0:1, 0:total_rows]
    for part in parts[1:]:
        total = total + part[0:1, 0:total_rows]
    place = lax.broadcasted_iota(jnp.int32, (1, total_rows), 1)
    scale = jnp.where(place < total_batch + fill, 1.0 / total, 0.0)
    scale_ref[...] = term_rows(scale)
    col_ref[...] = jnp.zeros_like(col_ref)
    spare_ref[...] = jnp.zeros_like(spare_ref)

    head = 3 * BLOCK // 4

    def add(index):
        start = pl.multiple_of(index * BLOCK, BLOCK)
        rows, rest = pl.ds(start, head), pl.ds(pl.multiple_of(start + head, 128), BLOCK - head)
        col_ref[...] += jnp.dot(scale_ref[:, rows], mass_ref[rows, :], preferred_element_type=f32)
        high, middle, low = (scale_ref[i : i + 1, rest].astype(f32) for i in range(3))
        factor = jnp.transpose(jnp.broadcast_to(high + middle + low, (128, BLOCK - head)), (1, 0))
        for low in range(0, mass_ref.shape[1], 128):
            part = mass_ref[rest, low : low + 128].astype(f32) * factor
            spare_ref[:, low : low + 128] += jnp.sum(part.reshape((BLOCK - head) // 8, 8, 128), axis=0)

    def crops(index, carry):
        if make is not None:
            make(index)
        add(index)
        return carry

    def queue(index, carry):
        if ready is not None:
            ready(index)
        add(total_batch // BLOCK + index)
        return carry

    lax.fori_loop(0, total_batch // BLOCK, crops, 0)
    lax.fori_loop(0, live_blocks(fill), queue, 0)
    return 1.0 / (sum_terms(col_ref[...]) + jnp.sum(spare_ref[...], axis=0, keepdims=True))


def sweep_kernel(total_batch, fill_ref, mass_in, batch_ref, columns_ref, *refs):
    *parts, sums_ref, mass_ref, scale_ref, col_ref, spare_ref, sems = refs
    fill = fill_ref[0]
    width = columns_ref.shape[1]

    def fetch(index):
        rows = pl.ds(pl.multiple_of(total_batch + index * BLOCK, BLOCK), BLOCK)
        return pltpu.make_async_copy(mass_in.at[rows, :], mass_ref.at[rows, :], sems.at[index])

    def start(index, carry):
        fetch(index).start()
        return carry

    lax.fori_loop(0, live_blocks(fill), start, 0)

    def make(index):
        rows = pl.ds(pl.multiple_of(index * BLOCK, BLOCK), BLOCK)
        crops = batch_ref[rows, :]
        for low in range(0, width, WIDE):
            scores = jnp.dot(crops, columns_ref[:, low : low + WIDE], preferred_element_type=f32)
            soft = jnp.exp2(scores * SOFT_SCALE)
            mass_ref[rows, low : low + WIDE] = (soft * soft).astype(bf16)

    column = column_factor(
        fill, total_batch, parts, mass_ref, scale_ref, col_ref, spare_ref, make, lambda index: fetch(index).wait()
    )
    sums_ref[...] = jnp.zeros_like(sums_ref)
    row_sums(term_rows(column), total_batch, live_blocks(fill), mass_ref, sums_ref)


def last_kernel(total_batch, fill_ref, side_ref, mass_ref, *refs):
    *parts, sums_ref, column_ref, scale_ref, col_ref, spare_ref = refs
    fill = fill_ref[0]
    column = column_factor(fill, total_batch, parts, mass_ref, scale_ref, col_ref, spare_ref)
    column_ref[...] = column
    sums_ref[0:1, total_batch:] = side_ref[...]
    row_sums(term_rows(column), total_batch, 0, mass_ref, sums_ref, BLOCK)


def slope_kernel(crop_count, first, last, batch_ref, columns_ref, column_ref, *refs):
    *parts, normed_out, grad_ref, loss_ref, back_ref, normed_ref, sems = refs
    total_batch, width = batch_ref.shape[0], last - first
    rows = ROWS
    wide = min(width, WIDE)
    grad_ref[...] = jnp.zeros_like(grad_ref)
    loss_ref[...] = jnp.zeros_like(loss_ref)

    bound = functools.reduce(jnp.add, [part[0:1, 2 * total_batch :] for part in parts])
    bound = 20.0 * bound + 1e-30
    back_ref[...] = jnp.broadcast_to(bound / 32768.0, (8, 128))
    scale = jnp.concatenate([32768.0 / bound] * (batch_ref.shape[1] // 128), axis=1)

    def keep(index):
        place = pl.ds(pl.multiple_of(index * rows, rows), rows)
        return pltpu.make_async_copy(normed_ref.at[place, :], normed_out.at[place, :], sems.at[index])

    def one(index, carry):
        start = pl.multiple_of(index * rows, rows)
        here = pl.ds(start, rows)

        later = pl.ds(pl.multiple_of(total_batch + start, rows), rows)
        code, soft_line = parts[0][0:1, here], parts[0][0:1, later]
        for part in parts[1:]:
            code, soft_line = code + part[0:1, here], soft_line + part[0:1, later]
        lines = [1.0 / ((crop_count - 1) * code), 10.0 / soft_line, jnp.log(soft_line)]
        factors = jnp.transpose(jnp.concatenate(lines + [jnp.zeros((125, rows), f32)], axis=0), (1, 0))
        code_factor, soft_factor, log_soft = (factors[:, i : i + 1] for i in range(3))
        crops = batch_ref[here, :]
        crops_t = jnp.transpose(crops.astype(f32), (1, 0)).astype(bf16)
        normed = jnp.zeros((rows, crops.shape[1]), f32)
        loss = jnp.zeros((8, 128), f32)
        for low in range(0, width, wide):
            place = slice(first + low, first + low + wide)
            columns = columns_ref[:, place]
            scores = jnp.dot(crops, columns, preferred_element_type=f32)
            soft = jnp.exp2(scores * SOFT_SCALE)
            assigned = (soft * soft) * column_ref[0:1, place] * code_factor
            slabs = assigned.reshape(rows // 128, crop_count, 128 // crop_count, wide)
            grouped = jnp.sum(slabs, axis=1, keepdims=True)
            targets = (grouped - slabs).reshape(rows, wide)
            logits = (soft * soft_factor - targets * 10.0).astype(bf16)
            terms = targets * (log_soft - scores * 10.0)
            folded = jnp.sum(terms.reshape(rows // 8, 8, wide), axis=0)
            for lane in range(0, wide, 128):
                loss = loss + folded[:, lane : lane + 128]
            grad_ref[:, low : low + wide] += jnp.dot(crops_t, logits, preferred_element_type=f32)
            normed = normed + dot_nt(logits, columns)
        normed_ref[here, :] = normed * scale
        keep(index).start()
        loss_ref[...] += loss
        return carry

    lax.fori_loop(0, total_batch // rows, one, 0)

    loss = jnp.maximum(jnp.sum(loss_ref[...]), 1e-30)
    exponent = jnp.floor(jnp.log2(jnp.full((1, 128), loss, f32)))
    mantissa = loss / jnp.exp2(exponent)
    high = jnp.floor(mantissa * 1024.0) / 1024.0
    lane = lax.broadcasted_iota(jnp.int32, (1, 128), 1)
    loss_ref[...] = jnp.broadcast_to(
        jnp.where(lane == 0, exponent, jnp.where(lane == 1, high, (mantissa - high) * 2048.0)), (8, 128)
    )

    def kept(index, carry):
        keep(index).wait()
        return carry

    lax.fori_loop(0, total_batch // rows, kept, 0)


def finish_kernel(piece_count, proto_ref, embed_ref, order_ref, back_ref, *refs):
    *pieces, out_ref, loss_ref, sorted_ref = refs
    rows = embed_ref.shape[0]
    size = rows // piece_count
    proto = proto_ref[0]
    for index, piece in enumerate(pieces):
        other = proto ^ index
        place = (other % 2) * (piece_count // 2) + other // 2
        sorted_ref[pl.ds(pl.multiple_of(place * size, size), size), :] = piece[0:size, :]
    loss_ref[0] = jnp.max(functools.reduce(jnp.add, [piece[size:, 0:128] for piece in pieces]))
    order = order_ref[...]
    high, middle, low = bf16_terms(sorted_ref[...])
    grad = dot_tn(order, high) + dot_tn(order, middle) + dot_tn(order, low)
    grad = grad * back_ref[0:1, 0:1]
    exact, inverse = unit_rows(embed_ref[...])
    out_ref[...] = inverse * (grad - exact * jnp.sum(exact * grad, axis=1, keepdims=True))


def solution(mesh):
    row_count, proto_count = mesh.shape["row"], mesh.shape["proto"]
    z_count = min(4, row_count)
    y_count = row_count // z_count
    x_count = proto_count // 2

    def shift_row(values, z, y):
        offset = z * y_count + y
        return lax.ppermute(values, "row", [(i, i ^ offset) for i in range(row_count)])

    def shift_proto(values, offset):
        return lax.ppermute(values, "proto", [(i, i ^ offset) for i in range(proto_count)])

    def shift_xy(values, x, y):
        pairs = []
        for i in range(row_count):
            for j in range(proto_count):
                pairs.append((i * proto_count + j, (i ^ y) * proto_count + (j ^ (2 * x))))
        return lax.ppermute(values, ("row", "proto"), pairs)

    def all_sum_parts(values):
        values = values + shift_proto(values, 1)
        moved = [shift_xy(values, x, y) for y in range(y_count) for x in range(x_count) if x or y]
        values = functools.reduce(jnp.add, moved, values)
        return [values] + [shift_row(values, z, 0) for z in range(1, z_count)]

    def body(embeddings, queue_feats, prototypes, crop_image, fill_count):
        batch_rows, feat = embeddings.shape
        queue_rows = queue_feats.shape[0]
        share, queue_share = batch_rows // proto_count, queue_rows // proto_count
        half = batch_rows // 2
        total_batch, total_queue = batch_rows * row_count, queue_rows * row_count
        total_rows = total_batch + total_queue
        row, proto = lax.axis_index("row"), lax.axis_index("proto")
        core, x, y, z = proto % 2, proto // 2, row % y_count, row // y_count
        place = jnp.stack([row, proto]).astype(jnp.int32)
        unit_rows_count = share + queue_share

        unit, order = pl.pallas_call(
            prep_kernel,
            name="prep",
            out_shape=[
                jax.ShapeDtypeStruct((unit_rows_count, feat), bf16),
                jax.ShapeDtypeStruct((batch_rows, batch_rows), bf16),
            ],
            in_specs=[SMEM, VMEM, ANY, ANY],
            out_specs=[VMEM, VMEM],
            scratch_shapes=[
                pltpu.VMEM((batch_rows, feat), bf16),
                pltpu.VMEM((queue_rows, feat), bf16),
                pltpu.VMEM((batch_rows, feat), f32),
                pltpu.VMEM((queue_rows, feat), f32),
                pltpu.SemaphoreType.DMA((2,)),
            ],
            compiler_params=limit(56),
        )(place, crop_image.reshape(1, batch_rows), embeddings, queue_feats)

        lines = jnp.stack([unit] + [shift_row(unit, z, 0) for z in range(1, z_count)])
        width = prototypes.shape[1] // row_count
        blocks = prototypes.reshape(-1, row_count, width).transpose(1, 0, 2)
        lines, blocks = lax.optimization_barrier((lines, blocks))
        columns = lax.all_to_all(blocks, "row", split_axis=0, concat_axis=0, tiled=True).reshape(feat, width)

        offsets, units = [], []
        for dy in range(y_count):
            there = shift_row(lines, 0, dy) if dy else lines
            for dx in range(x_count):
                moved = shift_proto(there, 2 * dx) if dx else there
                offsets += [(dy, 2 * dx), (dy, 2 * dx + 1)]
                units += [moved, shift_proto(moved, 1)]

        mass, sums, side, batch = pl.pallas_call(
            functools.partial(make_kernel, offsets, share, total_batch),
            name="make_mass",
            out_shape=[
                jax.ShapeDtypeStruct((total_rows, width), bf16),
                jax.ShapeDtypeStruct((1, total_rows), f32),
                jax.ShapeDtypeStruct((1, total_batch + 128), f32),
                jax.ShapeDtypeStruct((total_batch, feat), bf16),
            ],
            in_specs=[SMEM, SMEM, VMEM] + [ANY] * len(units),
            out_specs=[ANY, VMEM, VMEM, VMEM],
            scratch_shapes=[
                pltpu.VMEM((total_rows, width), bf16),
                pltpu.VMEM((total_queue, feat), bf16),
                pltpu.VMEM((8, width), f32),
                pltpu.SemaphoreType.DMA((len(units), z_count, 2)),
                pltpu.SemaphoreType.DMA,
            ],
            compiler_params=limit(56),
        )(place, fill_count, columns, *units)

        vectors = [pltpu.VMEM((8, total_rows), bf16), pltpu.VMEM((8, width), f32), pltpu.VMEM((8, width), f32)]
        sums = pl.pallas_call(
            functools.partial(sweep_kernel, total_batch),
            name="sweep",
            out_shape=jax.ShapeDtypeStruct((1, total_rows), f32),
            in_specs=[SMEM, ANY] + [VMEM] * (2 + z_count),
            out_specs=VMEM,
            scratch_shapes=[pltpu.VMEM((total_rows, width), bf16)]
            + vectors
            + [pltpu.SemaphoreType.DMA((total_queue // BLOCK,))],
            compiler_params=limit(30),
        )(fill_count, mass, batch, columns, *all_sum_parts(sums))

        code_sums, column = pl.pallas_call(
            functools.partial(last_kernel, total_batch),
            name="last_sweep",
            out_shape=[
                jax.ShapeDtypeStruct((1, 2 * total_batch + 128), f32),
                jax.ShapeDtypeStruct((1, width), f32),
            ],
            in_specs=[SMEM] + [VMEM] * (2 + z_count),
            out_specs=[VMEM, VMEM],
            scratch_shapes=vectors,
            compiler_params=limit(8),
        )(fill_count, side, mass, *all_sum_parts(sums))

        code_parts = all_sum_parts(code_sums)

        def slopes(first, last, batch):
            return pl.pallas_call(
                functools.partial(slope_kernel, CROPS, first, last),
                name="slopes",
                out_shape=[
                    jax.ShapeDtypeStruct((total_batch, feat), f32),
                    jax.ShapeDtypeStruct((feat, last - first), f32),
                    jax.ShapeDtypeStruct((8, 128), f32),
                    jax.ShapeDtypeStruct((8, 128), f32),
                ],
                in_specs=[VMEM] * (3 + z_count),
                out_specs=[ANY, VMEM, VMEM, VMEM],
                scratch_shapes=[
                    pltpu.VMEM((total_batch, feat), f32),
                    pltpu.SemaphoreType.DMA((total_batch // ROWS,)),
                ],
                compiler_params=limit(24),
            )(batch, columns, column, *code_parts)

        def as_blocks(grad_columns):
            return grad_columns.astype(f16).reshape(row_count, feat // row_count, -1)

        def exchange(blocks):
            return lax.all_to_all(blocks, "row", split_axis=0, concat_axis=0, tiled=True)

        normed_part, grad_columns, loss, back = slopes(0, width, batch)
        size = half // x_count

        def pick(values, index, axis):
            return lax.dynamic_index_in_dim(values, index, axis, keepdims=False)

        pieces = normed_part.reshape(z_count, y_count, 2, x_count, size, feat)

        away = shift_proto(pick(pieces, 1 - core, 2).astype(f16), 1)
        kept = pick(pieces, core, 2) + away.astype(f32)
        total = None
        for dy in range(y_count):
            for dx in range(x_count):
                part = pick(pick(kept, x ^ dx, 2), y ^ dy, 1)
                if dx or dy:
                    part = shift_xy(part.astype(f16), dx, dy).astype(f32)
                total = part if total is None else total + part
        arriving = [shift_row(pick(total, z ^ dz, 0).astype(f16), dz, 0) for dz in range(1, z_count)]

        sent = jnp.concatenate([as_blocks(grad_columns), jnp.broadcast_to(loss[0:1].astype(f16), (row_count, feat // row_count, 128))], axis=2)
        got = exchange(sent)
        grad_proto = got[:, :, :width].astype(f32)
        grad_proto = grad_proto.transpose(1, 0, 2).reshape(feat // row_count, row_count * width)
        code = got[:, 0, width:].astype(f32)
        losses = jnp.sum((code[:, 1] + code[:, 2] / 2048.0) * jnp.exp2(code[:, 0])) / total_batch
        *arriving, losses = lax.optimization_barrier((*arriving, losses))
        piece = functools.reduce(jnp.add, [part.astype(f32) for part in arriving], pick(total, z, 0))
        piece = jnp.concatenate([piece, jnp.full((8, feat), losses, f32)], axis=0)

        gathered = [piece] + [shift_proto(piece, k) for k in range(1, proto_count)]
        grad_embed, loss = pl.pallas_call(
            functools.partial(finish_kernel, proto_count),
            name="finish",
            out_shape=[
                jax.ShapeDtypeStruct((batch_rows, feat), f32),
                jax.ShapeDtypeStruct((1,), f32),
            ],
            in_specs=[SMEM] + [VMEM] * (3 + proto_count),
            out_specs=[VMEM, SMEM],
            scratch_shapes=[pltpu.VMEM((batch_rows, feat), f32)],
            compiler_params=limit(8),
        )(proto.reshape(1).astype(jnp.int32), embeddings, order, back, *gathered)
        return grad_embed, grad_proto, loss

    placed = (P("row", None), P("row", None), P("row", "proto"), P("row"), P())
    return jax.shard_map(
        body,
        mesh=mesh,
        in_specs=placed,
        out_specs=(P("row", None), P("row", "proto"), P()),
        check_vma=False,
    )
```

```python
import functools

import jax
import jax.numpy as jnp
from jax import lax
from jax.experimental import pallas as pl
from jax.experimental.pallas import tpu as pltpu
from jax.sharding import PartitionSpec as P

CROPS = 8
LOG2E = 1.4426950408889634
SOFT_SCALE = 10.0 * LOG2E
BLOCK = 1024
WIDE = 256
ROWS = 1024

f32 = jnp.float32
bf16 = jnp.bfloat16
f16 = jnp.float16

VMEM = pl.BlockSpec(memory_space=pltpu.VMEM)
SMEM = pl.BlockSpec(memory_space=pltpu.SMEM)
ANY = pl.BlockSpec(memory_space=pl.ANY)


def limit(mib):
    return pltpu.CompilerParams(vmem_limit_bytes=mib << 20)


def bf16_terms(values):
    high = values.astype(bf16)
    rest = values - high.astype(f32)
    middle = rest.astype(bf16)
    return high, middle, (rest - middle.astype(f32)).astype(bf16)


def term_rows(values):
    high, middle, low = bf16_terms(values)
    return jnp.concatenate([high, middle, low] + [jnp.zeros_like(high)] * 5, axis=0)


def sum_terms(products):
    return products[0:1] + products[1:2] + products[2:3]


def dot_nt(left, right):
    return lax.dot_general(left, right, (((1,), (1,)), ((), ())), preferred_element_type=f32)


def dot_tn(left, right):
    return lax.dot_general(left, right, (((0,), (0,)), ((), ())), preferred_element_type=f32)


def unit_rows(raw):
    values = raw.astype(f32)
    inverse = lax.rsqrt(jnp.sum(values * values, axis=1, keepdims=True) + 1e-06)
    return values * inverse, inverse


def prep_kernel(
    place_ref, image_ref, embed_in, queue_in, unit_ref, order_ref, embed_ref, queue_ref, sorted_ref, queued_ref, sems
):
    fetch = [
        pltpu.make_async_copy(embed_in, embed_ref, sems.at[0]),
        pltpu.make_async_copy(queue_in, queue_ref, sems.at[1]),
    ]
    for copy in fetch:
        copy.start()
    row, proto = place_ref[0], place_ref[1]
    rows = embed_ref.shape[0]
    half = rows // 2
    images = half // CROPS
    local = image_ref[...] - row * (rows // CROPS)
    across = jnp.broadcast_to(local, (rows, rows)).astype(f32)
    down = jnp.transpose(across, (1, 0))
    first = lax.broadcasted_iota(jnp.int32, (rows, rows), 0)
    second = lax.broadcasted_iota(jnp.int32, (rows, rows), 1)
    earlier = jnp.where((across == down) & (first < second), 1.0, 0.0)
    rank = jnp.sum(earlier, axis=0, keepdims=True).astype(jnp.int32)
    upper = jnp.where(local >= images, 1, 0)
    position = upper * half + rank * images + (local - upper * images)
    order = (first == position).astype(f32).astype(bf16)
    order_ref[...] = order
    for copy in fetch:
        copy.wait()
    normed = unit_rows(embed_ref[...])[0].astype(bf16)
    sorted_ref[...] = jnp.dot(order, normed, preferred_element_type=f32)
    queued_ref[...] = unit_rows(queue_ref[...])[0]
    share = rows * unit_ref.shape[0] // (rows + queue_ref.shape[0])
    queue_share = unit_ref.shape[0] - share
    unit_ref[0:share, :] = sorted_ref[pl.ds(pl.multiple_of(proto * share, share), share), :].astype(bf16)
    unit_ref[share:, :] = queued_ref[
        pl.ds(pl.multiple_of(proto * queue_share, queue_share), queue_share), :
    ].astype(bf16)


def row_sums(column, total_batch, queue_blocks, mass_ref, out_ref, wide=None):
    head = wide or BLOCK // 4
    width = mass_ref.shape[1]
    step = 128
    factor = column[0:1]
    ones = jnp.ones((8, 128), bf16)

    def one(index, carry):
        start = pl.multiple_of(index * BLOCK, BLOCK)
        out_ref[0:1, pl.ds(start, head)] = sum_terms(dot_nt(column, mass_ref[pl.ds(start, head), :]))
        for rows in range(head, BLOCK, step):
            here = pl.ds(pl.multiple_of(start + rows, step), step)
            total = None
            for low in range(0, width, 256):
                pair = mass_ref[here, low : low + 128] * factor[:, low : low + 128]
                pair += mass_ref[here, low + 128 : low + 256] * factor[:, low + 128 : low + 256]
                total = pair.astype(f32) if total is None else total + pair.astype(f32)
            high = total.astype(bf16)
            low = (total - high.astype(f32)).astype(bf16)
            out_ref[0:1, here] = (dot_nt(ones, high) + dot_nt(ones, low))[0:1]
        return carry

    lax.fori_loop(0, total_batch // BLOCK + queue_blocks, one, 0)


def kept_places(total_rows, total_batch, feat, width):
    across = width // feat
    pieces = [
        (total_rows + feat * (1 + index // across), feat * (index % across), feat * index)
        for index in range(total_batch // feat)
    ]
    return total_rows, pieces


def live_blocks(fill):
    return lax.div(fill + (BLOCK - 1), BLOCK)


def make_kernel(offsets, share, total_batch, place_ref, fill_ref, *refs):
    *inputs, mass_out, sums_ref, side_ref, batch_ref, columns_ref, mass_ref, queue_ref, col_ref, sems, strip_sems, kept_sems, out_sems = refs
    *units, strips_ref = inputs
    row, proto = place_ref[0], place_ref[1]
    fill = fill_ref[0]
    z_count, unit_rows_count, _ = units[0].shape
    queue_share = unit_rows_count - share
    proto_count = 1 + max(other for _, other in offsets)
    y_count = 1 + max(y for y, _ in offsets)
    strip_copies = []
    z_count, y_count, features, _ = strips_ref.shape
    for z in range(z_count):
        for y in range(y_count):
            first = pl.multiple_of((z * y_count + (lax.rem(row, y_count) ^ y)) * features, features)
            strip_copies.append(
                pltpu.make_async_copy(
                    strips_ref.at[z, y], columns_ref.at[pl.ds(first, features), :], strip_sems.at[z, y]
                )
            )
    for copy in strip_copies:
        copy.start()
    copies = []
    for index, (unit, (y, other)) in enumerate(zip(units, offsets)):
        for z in range(z_count):
            place = (row ^ (z * y_count + y)) * proto_count + (proto ^ other)
            crops = pl.multiple_of(place * share, share)
            queued = pl.multiple_of(place * queue_share, queue_share)
            copies.append(
                pltpu.make_async_copy(
                    unit.at[z, pl.ds(0, share), :],
                    batch_ref.at[pl.ds(crops, share), :],
                    sems.at[index, z, 0],
                )
            )
            copies.append(
                pltpu.make_async_copy(
                    unit.at[z, pl.ds(share, queue_share), :],
                    queue_ref.at[pl.ds(queued, queue_share), :],
                    sems.at[index, z, 1],
                )
            )
    for copy in copies[0::2] + copies[1::2]:
        copy.start()
    total_queue = queue_ref.shape[0]
    total_rows = total_batch + total_queue
    width = columns_ref.shape[1]
    col_ref[...] = jnp.zeros_like(col_ref)
    sums_ref[...] = jnp.zeros_like(sums_ref)
    ones = jnp.ones((8, 128), bf16)
    for copy in strip_copies:
        copy.wait()
    bound = jnp.max(jnp.abs(columns_ref[...].astype(f32)))
    side_ref[0:1, total_batch:] = jnp.full((1, 128), bound, f32)
    for copy in copies[0::2]:
        copy.wait()

    def add_columns(low, mass):
        col_ref[:, low : low + WIDE] += jnp.sum(mass.reshape(BLOCK // 8, 8, WIDE), axis=0)

    feat = columns_ref.shape[0]
    first, pieces = kept_places(total_rows, total_batch, feat, width)
    kept = [pltpu.make_async_copy(columns_ref, mass_out.at[pl.ds(first, feat), :], kept_sems.at[0])]
    for index, (place, lane, crop) in enumerate(pieces):
        kept.append(
            pltpu.make_async_copy(
                batch_ref.at[pl.ds(crop, feat), :],
                mass_out.at[pl.ds(place, feat), pl.ds(lane, feat)],
                kept_sems.at[1 + index],
            )
        )
    for copy in kept:
        copy.start()

    def keep(start):
        place = pl.ds(pl.multiple_of(start, BLOCK), BLOCK)
        return pltpu.make_async_copy(mass_ref.at[place, :], mass_out.at[place, :], out_sems)

    def crops_block(index, carry):
        start = pl.multiple_of(index * BLOCK, BLOCK)
        rows = batch_ref[pl.ds(start, BLOCK), :]
        lanes = None
        for low in range(0, width, WIDE):
            scores = jnp.dot(rows, columns_ref[:, low : low + WIDE], preferred_element_type=f32)
            soft = jnp.exp2(scores * SOFT_SCALE)
            mass = soft * soft
            mass_ref[pl.ds(start, BLOCK), low : low + WIDE] = mass.astype(bf16)
            add_columns(low, mass)
            for lane in range(0, WIDE, 128):
                part = soft[:, lane : lane + 128]
                lanes = part if lanes is None else lanes + part
        high, middle, small = bf16_terms(lanes)
        total = dot_nt(ones, high) + dot_nt(ones, middle) + dot_nt(ones, small)
        side_ref[0:1, pl.ds(start, BLOCK)] = total[0:1]
        keep(start).start()
        return carry

    lax.fori_loop(0, total_batch // BLOCK, crops_block, 0)

    for copy in copies[1::2]:
        copy.wait()

    def queue_block(index, masked):
        start = pl.multiple_of(index * BLOCK, BLOCK)
        rows = queue_ref[pl.ds(start, BLOCK), :]
        place = pl.ds(pl.multiple_of(total_batch + start, BLOCK), BLOCK)
        for low in range(0, width, WIDE):
            scores = jnp.dot(rows, columns_ref[:, low : low + WIDE], preferred_element_type=f32)
            soft = jnp.exp2(scores * SOFT_SCALE)
            mass = soft * soft
            if masked:
                live = lax.broadcasted_iota(jnp.int32, (BLOCK, WIDE), 0) < fill - start
                mass = jnp.where(live, mass, 0.0)
            mass_ref[place, low : low + WIDE] = mass.astype(bf16)
            add_columns(low, mass)
        keep(total_batch + start).start()

    def whole_block(index, carry):
        queue_block(index, False)
        return carry

    whole = lax.div(fill, BLOCK)
    lax.fori_loop(0, whole, whole_block, 0)

    @pl.when(live_blocks(fill) > whole)
    def _():
        queue_block(whole, True)

    column = term_rows(1.0 / jnp.sum(col_ref[...], axis=0, keepdims=True))
    row_sums(column, total_batch, live_blocks(fill), mass_ref, sums_ref)

    def finish(index, carry):
        keep(index * BLOCK).wait()
        return carry

    lax.fori_loop(0, total_batch // BLOCK + live_blocks(fill), finish, 0)
    for copy in kept:
        copy.wait()


def column_factor(fill, total_batch, parts, mass_ref, scale_ref, col_ref, spare_ref, make=None, ready=None):
    total_rows = scale_ref.shape[1]
    total = parts[0][0:1, 0:total_rows]
    for part in parts[1:]:
        total = total + part[0:1, 0:total_rows]
    place = lax.broadcasted_iota(jnp.int32, (1, total_rows), 1)
    scale = jnp.where(place < total_batch + fill, 1.0 / total, 0.0)
    scale_ref[...] = term_rows(scale)
    col_ref[...] = jnp.zeros_like(col_ref)
    spare_ref[...] = jnp.zeros_like(spare_ref)

    head = 3 * BLOCK // 4

    def add(index):
        start = pl.multiple_of(index * BLOCK, BLOCK)
        rows, rest = pl.ds(start, head), pl.ds(pl.multiple_of(start + head, 128), BLOCK - head)
        col_ref[...] += jnp.dot(scale_ref[:, rows], mass_ref[rows, :], preferred_element_type=f32)
        high, middle, low = (scale_ref[i : i + 1, rest].astype(f32) for i in range(3))
        factor = jnp.transpose(jnp.broadcast_to(high + middle + low, (128, BLOCK - head)), (1, 0))
        for low in range(0, mass_ref.shape[1], 128):
            part = mass_ref[rest, low : low + 128].astype(f32) * factor
            spare_ref[:, low : low + 128] += jnp.sum(part.reshape((BLOCK - head) // 8, 8, 128), axis=0)

    def crops(index, carry):
        if make is not None:
            make(index)
        add(index)
        return carry

    def queue(index, carry):
        if ready is not None:
            ready(index)
        add(total_batch // BLOCK + index)
        return carry

    lax.fori_loop(0, total_batch // BLOCK, crops, 0)
    lax.fori_loop(0, live_blocks(fill), queue, 0)
    return 1.0 / (sum_terms(col_ref[...]) + jnp.sum(spare_ref[...], axis=0, keepdims=True))


def sweep_kernel(total_batch, fill_ref, mass_in, *refs):
    *parts, sums_ref, mass_ref, scale_ref, col_ref, spare_ref, batch_ref, columns_ref, sems, kept_sems = refs
    fill = fill_ref[0]
    feat, width = columns_ref.shape
    first, pieces = kept_places(mass_ref.shape[0], total_batch, feat, width)
    kept = [pltpu.make_async_copy(mass_in.at[pl.ds(first, feat), :], columns_ref, kept_sems.at[0])]
    for index, (place, lane, crop) in enumerate(pieces):
        kept.append(
            pltpu.make_async_copy(
                mass_in.at[pl.ds(place, feat), pl.ds(lane, feat)],
                batch_ref.at[pl.ds(crop, feat), :],
                kept_sems.at[1 + index],
            )
        )
    for copy in kept:
        copy.start()

    def fetch(index):
        rows = pl.ds(pl.multiple_of(total_batch + index * BLOCK, BLOCK), BLOCK)
        return pltpu.make_async_copy(mass_in.at[rows, :], mass_ref.at[rows, :], sems.at[index])

    def start(index, carry):
        fetch(index).start()
        return carry

    lax.fori_loop(0, live_blocks(fill), start, 0)

    for copy in kept:
        copy.wait()

    def make(index):
        rows = pl.ds(pl.multiple_of(index * BLOCK, BLOCK), BLOCK)
        crops = batch_ref[rows, :]
        for low in range(0, width, WIDE):
            scores = jnp.dot(crops, columns_ref[:, low : low + WIDE], preferred_element_type=f32)
            soft = jnp.exp2(scores * SOFT_SCALE)
            mass_ref[rows, low : low + WIDE] = (soft * soft).astype(bf16)

    column = column_factor(
        fill, total_batch, parts, mass_ref, scale_ref, col_ref, spare_ref, make, lambda index: fetch(index).wait()
    )
    sums_ref[...] = jnp.zeros_like(sums_ref)
    row_sums(term_rows(column), total_batch, live_blocks(fill), mass_ref, sums_ref)


def last_kernel(total_batch, fill_ref, side_ref, mass_ref, *refs):
    *parts, sums_ref, column_ref, scale_ref, col_ref, spare_ref = refs
    fill = fill_ref[0]
    column = column_factor(fill, total_batch, parts, mass_ref, scale_ref, col_ref, spare_ref)
    column_ref[...] = column
    sums_ref[0:1, total_batch:] = side_ref[...]
    row_sums(term_rows(column), total_batch, 0, mass_ref, sums_ref, BLOCK)


def slope_kernel(crop_count, first, last, batch_ref, columns_ref, column_ref, *refs):
    *parts, normed_out, grad_ref, loss_ref, back_ref, normed_ref, sems = refs
    total_batch, width = batch_ref.shape[0], last - first
    rows = ROWS
    wide = min(width, WIDE)
    grad_ref[...] = jnp.zeros_like(grad_ref)
    loss_ref[...] = jnp.zeros_like(loss_ref)

    bound = functools.reduce(jnp.add, [part[0:1, 2 * total_batch :] for part in parts])
    bound = 20.0 * bound + 1e-30
    back_ref[...] = jnp.broadcast_to(bound / 32768.0, (8, 128))
    scale = jnp.concatenate([32768.0 / bound] * (batch_ref.shape[1] // 128), axis=1)

    def keep(index):
        place = pl.ds(pl.multiple_of(index * rows, rows), rows)
        return pltpu.make_async_copy(normed_ref.at[place, :], normed_out.at[place, :], sems.at[index])

    def one(index, carry):
        start = pl.multiple_of(index * rows, rows)
        here = pl.ds(start, rows)

        later = pl.ds(pl.multiple_of(total_batch + start, rows), rows)
        code, soft_line = parts[0][0:1, here], parts[0][0:1, later]
        for part in parts[1:]:
            code, soft_line = code + part[0:1, here], soft_line + part[0:1, later]
        lines = [1.0 / ((crop_count - 1) * code), 10.0 / soft_line, jnp.log(soft_line)]
        factors = jnp.transpose(jnp.concatenate(lines + [jnp.zeros((125, rows), f32)], axis=0), (1, 0))
        code_factor, soft_factor, log_soft = (factors[:, i : i + 1] for i in range(3))
        crops = batch_ref[here, :]
        crops_t = jnp.transpose(crops.astype(f32), (1, 0)).astype(bf16)
        normed = jnp.zeros((rows, crops.shape[1]), f32)
        loss = jnp.zeros((8, 128), f32)
        for low in range(0, width, wide):
            place = slice(first + low, first + low + wide)
            columns = columns_ref[:, place]
            scores = jnp.dot(crops, columns, preferred_element_type=f32)
            soft = jnp.exp2(scores * SOFT_SCALE)
            assigned = (soft * soft) * column_ref[0:1, place] * code_factor
            slabs = assigned.reshape(rows // 128, crop_count, 128 // crop_count, wide)
            grouped = jnp.sum(slabs, axis=1, keepdims=True)
            targets = (grouped - slabs).reshape(rows, wide)
            logits = (soft * soft_factor - targets * 10.0).astype(bf16)
            terms = targets * (log_soft - scores * 10.0)
            folded = jnp.sum(terms.reshape(rows // 8, 8, wide), axis=0)
            for lane in range(0, wide, 128):
                loss = loss + folded[:, lane : lane + 128]
            grad_ref[:, low : low + wide] += jnp.dot(crops_t, logits, preferred_element_type=f32)
            normed = normed + dot_nt(logits, columns)
        normed_ref[here, :] = normed * scale
        keep(index).start()
        loss_ref[...] += loss
        return carry

    lax.fori_loop(0, total_batch // rows, one, 0)

    loss = jnp.maximum(jnp.sum(loss_ref[...]), 1e-30)
    exponent = jnp.floor(jnp.log2(jnp.full((1, 128), loss, f32)))
    mantissa = loss / jnp.exp2(exponent)
    high = jnp.floor(mantissa * 1024.0) / 1024.0
    lane = lax.broadcasted_iota(jnp.int32, (1, 128), 1)
    loss_ref[...] = jnp.broadcast_to(
        jnp.where(lane == 0, exponent, jnp.where(lane == 1, high, (mantissa - high) * 2048.0)), (8, 128)
    )

    def kept(index, carry):
        keep(index).wait()
        return carry

    lax.fori_loop(0, total_batch // rows, kept, 0)


def finish_kernel(piece_count, proto_ref, embed_ref, order_ref, back_ref, *refs):
    *pieces, out_ref, loss_ref, sorted_ref = refs
    rows = embed_ref.shape[0]
    size = rows // piece_count
    proto = proto_ref[0]
    for index, piece in enumerate(pieces):
        other = proto ^ index
        place = (other % 2) * (piece_count // 2) + other // 2
        sorted_ref[pl.ds(pl.multiple_of(place * size, size), size), :] = piece[0:size, :]
    loss_ref[0] = jnp.max(functools.reduce(jnp.add, [piece[size:, 0:128] for piece in pieces]))
    order = order_ref[...]
    high, middle, low = bf16_terms(sorted_ref[...])
    grad = dot_tn(order, high) + dot_tn(order, middle) + dot_tn(order, low)
    grad = grad * back_ref[0:1, 0:1]
    exact, inverse = unit_rows(embed_ref[...])
    out_ref[...] = inverse * (grad - exact * jnp.sum(exact * grad, axis=1, keepdims=True))


def solution(mesh):
    row_count, proto_count = mesh.shape["row"], mesh.shape["proto"]
    z_count = min(4, row_count)
    y_count = row_count // z_count
    x_count = proto_count // 2

    def shift_row(values, z, y):
        offset = z * y_count + y
        return lax.ppermute(values, "row", [(i, i ^ offset) for i in range(row_count)])

    def shift_proto(values, offset):
        return lax.ppermute(values, "proto", [(i, i ^ offset) for i in range(proto_count)])

    def shift_xy(values, x, y):
        pairs = []
        for i in range(row_count):
            for j in range(proto_count):
                pairs.append((i * proto_count + j, (i ^ y) * proto_count + (j ^ (2 * x))))
        return lax.ppermute(values, ("row", "proto"), pairs)

    def all_sum_parts(values):
        values = values + shift_proto(values, 1)
        moved = [shift_xy(values, x, y) for y in range(y_count) for x in range(x_count) if x or y]
        values = functools.reduce(jnp.add, moved, values)
        return [values] + [shift_row(values, z, 0) for z in range(1, z_count)]

    def body(embeddings, queue_feats, prototypes, crop_image, fill_count):
        batch_rows, feat = embeddings.shape
        queue_rows = queue_feats.shape[0]
        share, queue_share = batch_rows // proto_count, queue_rows // proto_count
        half = batch_rows // 2
        total_batch, total_queue = batch_rows * row_count, queue_rows * row_count
        total_rows = total_batch + total_queue
        row, proto = lax.axis_index("row"), lax.axis_index("proto")
        core, x, y, z = proto % 2, proto // 2, row % y_count, row // y_count
        place = jnp.stack([row, proto]).astype(jnp.int32)
        unit_rows_count = share + queue_share

        def pick(values, index, axis):
            return lax.dynamic_index_in_dim(values, index, axis, keepdims=False)

        unit, order = pl.pallas_call(
            prep_kernel,
            name="prep",
            out_shape=[
                jax.ShapeDtypeStruct((unit_rows_count, feat), bf16),
                jax.ShapeDtypeStruct((batch_rows, batch_rows), bf16),
            ],
            in_specs=[SMEM, VMEM, ANY, ANY],
            out_specs=[VMEM, VMEM],
            scratch_shapes=[
                pltpu.VMEM((batch_rows, feat), bf16),
                pltpu.VMEM((queue_rows, feat), bf16),
                pltpu.VMEM((batch_rows, feat), f32),
                pltpu.VMEM((queue_rows, feat), f32),
                pltpu.SemaphoreType.DMA((2,)),
            ],
            compiler_params=limit(56),
        )(place, crop_image.reshape(1, batch_rows), embeddings, queue_feats)

        lines = jnp.stack([unit] + [shift_row(unit, z, 0) for z in range(1, z_count)])
        width = prototypes.shape[1] // row_count
        features = prototypes.shape[0]

        def strip(dy):
            places = [((other * y_count) + (y ^ dy)) * width for other in range(z_count)]
            return jnp.stack([lax.dynamic_slice(prototypes, (0, place), (features, width)) for place in places])

        strips = [shift_row(strip(dy), 0, dy) if dy else strip(dy) for dy in range(y_count)]
        lanes = [[other * y_count + own for other in range(z_count)] for own in range(y_count)]
        lines, strips = lax.optimization_barrier((lines, jnp.stack(strips, axis=1)))
        strips = lax.all_to_all(
            strips, "row", split_axis=0, concat_axis=0, axis_index_groups=lanes, tiled=True
        )

        offsets, units = [], []
        for dy in range(y_count):
            there = shift_row(lines, 0, dy) if dy else lines
            for dx in range(x_count):
                moved = shift_proto(there, 2 * dx) if dx else there
                offsets += [(dy, 2 * dx), (dy, 2 * dx + 1)]
                units += [moved, shift_proto(moved, 1)]

        mass, sums, side, batch, columns = pl.pallas_call(
            functools.partial(make_kernel, offsets, share, total_batch),
            name="make_mass",
            out_shape=[
                jax.ShapeDtypeStruct((total_rows + feat * (1 + total_batch // width), width), bf16),
                jax.ShapeDtypeStruct((1, total_rows), f32),
                jax.ShapeDtypeStruct((1, total_batch + 128), f32),
                jax.ShapeDtypeStruct((total_batch, feat), bf16),
                jax.ShapeDtypeStruct((feat, width), bf16),
            ],
            in_specs=[SMEM, SMEM] + [ANY] * (len(units) + 1),
            out_specs=[ANY, VMEM, VMEM, VMEM, VMEM],
            scratch_shapes=[
                pltpu.VMEM((total_rows, width), bf16),
                pltpu.VMEM((total_queue, feat), bf16),
                pltpu.VMEM((8, width), f32),
                pltpu.SemaphoreType.DMA((len(units), z_count, 2)),
                pltpu.SemaphoreType.DMA((z_count, y_count)),
                pltpu.SemaphoreType.DMA((1 + total_batch // feat,)),
                pltpu.SemaphoreType.DMA,
            ],
            compiler_params=limit(53),
        )(place, fill_count, *units, strips)

        vectors = [pltpu.VMEM((8, total_rows), bf16), pltpu.VMEM((8, width), f32), pltpu.VMEM((8, width), f32)]
        sums = pl.pallas_call(
            functools.partial(sweep_kernel, total_batch),
            name="sweep",
            out_shape=jax.ShapeDtypeStruct((1, total_rows), f32),
            in_specs=[SMEM, ANY] + [VMEM] * z_count,
            out_specs=VMEM,
            scratch_shapes=[pltpu.VMEM((total_rows, width), bf16)]
            + vectors
            + [
                pltpu.VMEM((total_batch, feat), bf16),
                pltpu.VMEM((feat, width), bf16),
                pltpu.SemaphoreType.DMA((total_queue // BLOCK,)),
                pltpu.SemaphoreType.DMA((1 + total_batch // feat,)),
            ],
            compiler_params=limit(33),
        )(fill_count, mass, *all_sum_parts(sums))

        code_sums, column = pl.pallas_call(
            functools.partial(last_kernel, total_batch),
            name="last_sweep",
            out_shape=[
                jax.ShapeDtypeStruct((1, 2 * total_batch + 128), f32),
                jax.ShapeDtypeStruct((1, width), f32),
            ],
            in_specs=[SMEM] + [VMEM] * (2 + z_count),
            out_specs=[VMEM, VMEM],
            scratch_shapes=vectors,
            compiler_params=limit(8),
        )(fill_count, side, mass, *all_sum_parts(sums))

        code_parts = all_sum_parts(code_sums)

        def slopes(first, last, batch):
            return pl.pallas_call(
                functools.partial(slope_kernel, CROPS, first, last),
                name="slopes",
                out_shape=[
                    jax.ShapeDtypeStruct((total_batch, feat), f32),
                    jax.ShapeDtypeStruct((feat, last - first), f32),
                    jax.ShapeDtypeStruct((8, 128), f32),
                    jax.ShapeDtypeStruct((8, 128), f32),
                ],
                in_specs=[VMEM] * (3 + z_count),
                out_specs=[ANY, VMEM, VMEM, VMEM],
                scratch_shapes=[
                    pltpu.VMEM((total_batch, feat), f32),
                    pltpu.SemaphoreType.DMA((total_batch // ROWS,)),
                ],
                compiler_params=limit(24),
            )(batch, columns, column, *code_parts)

        def as_blocks(grad_columns):
            return grad_columns.astype(f16).reshape(row_count, feat // row_count, -1)

        def exchange(blocks):
            return lax.all_to_all(blocks, "row", split_axis=0, concat_axis=0, tiled=True)

        normed_part, grad_columns, loss, back = slopes(0, width, batch)
        size = half // x_count

        pieces = normed_part.reshape(z_count, y_count, 2, x_count, size, feat)

        away = shift_proto(pick(pieces, 1 - core, 2).astype(f16), 1)
        kept = pick(pieces, core, 2) + away.astype(f32)
        total = None
        for dy in range(y_count):
            for dx in range(x_count):
                part = pick(pick(kept, x ^ dx, 2), y ^ dy, 1)
                if dx or dy:
                    part = shift_xy(part.astype(f16), dx, dy).astype(f32)
                total = part if total is None else total + part
        arriving = [shift_row(pick(total, z ^ dz, 0).astype(f16), dz, 0) for dz in range(1, z_count)]

        sent = jnp.concatenate([as_blocks(grad_columns), jnp.broadcast_to(loss[0:1].astype(f16), (row_count, feat // row_count, 128))], axis=2)
        got = exchange(sent)
        grad_proto = got[:, :, :width].astype(f32)
        grad_proto = grad_proto.transpose(1, 0, 2).reshape(feat // row_count, row_count * width)
        code = got[:, 0, width:].astype(f32)
        losses = jnp.sum((code[:, 1] + code[:, 2] / 2048.0) * jnp.exp2(code[:, 0])) / total_batch
        *arriving, losses = lax.optimization_barrier((*arriving, losses))
        piece = functools.reduce(jnp.add, [part.astype(f32) for part in arriving], pick(total, z, 0))
        piece = jnp.concatenate([piece, jnp.full((8, feat), losses, f32)], axis=0)

        gathered = [piece] + [shift_proto(piece, k) for k in range(1, proto_count)]
        grad_embed, loss = pl.pallas_call(
            functools.partial(finish_kernel, proto_count),
            name="finish",
            out_shape=[
                jax.ShapeDtypeStruct((batch_rows, feat), f32),
                jax.ShapeDtypeStruct((1,), f32),
            ],
            in_specs=[SMEM] + [VMEM] * (3 + proto_count),
            out_specs=[VMEM, SMEM],
            scratch_shapes=[pltpu.VMEM((batch_rows, feat), f32)],
            compiler_params=limit(8),
        )(proto.reshape(1).astype(jnp.int32), embeddings, order, back, *gathered)
        return grad_embed, grad_proto, loss

    placed = (P("row", None), P("row", None), P("row", "proto"), P("row"), P())
    return jax.shard_map(
        body,
        mesh=mesh,
        in_specs=placed,
        out_specs=(P("row", None), P("row", "proto"), P()),
        check_vma=False,
    )
```

```python
import functools

import jax
import jax.numpy as jnp
from jax import lax
from jax.experimental import pallas as pl
from jax.experimental.pallas import tpu as pltpu
from jax.sharding import PartitionSpec as P

CROPS = 8
LOG2E = 1.4426950408889634
SOFT_SCALE = 10.0 * LOG2E
BLOCK = 1024
WIDE = 256
ROWS = 1024

f32 = jnp.float32
bf16 = jnp.bfloat16
f16 = jnp.float16

VMEM = pl.BlockSpec(memory_space=pltpu.VMEM)
SMEM = pl.BlockSpec(memory_space=pltpu.SMEM)
ANY = pl.BlockSpec(memory_space=pl.ANY)


def limit(mib):
    return pltpu.CompilerParams(vmem_limit_bytes=mib << 20)


def bf16_terms(values):
    high = values.astype(bf16)
    rest = values - high.astype(f32)
    middle = rest.astype(bf16)
    return high, middle, (rest - middle.astype(f32)).astype(bf16)


def term_rows(values):
    high, middle, low = bf16_terms(values)
    return jnp.concatenate([high, middle, low] + [jnp.zeros_like(high)] * 5, axis=0)


def sum_terms(products):
    return products[0:1] + products[1:2] + products[2:3]


def dot_nt(left, right):
    return lax.dot_general(left, right, (((1,), (1,)), ((), ())), preferred_element_type=f32)


def dot_tn(left, right):
    return lax.dot_general(left, right, (((0,), (0,)), ((), ())), preferred_element_type=f32)


def unit_rows(raw):
    values = raw.astype(f32)
    inverse = lax.rsqrt(jnp.sum(values * values, axis=1, keepdims=True) + 1e-06)
    return values * inverse, inverse


def prep_kernel(
    row_ref, proto_ref, image_ref, embed_in, queue_in, unit_ref, order_ref, embed_ref, queue_ref, sorted_ref, queued_ref, sems
):
    fetch = [
        pltpu.make_async_copy(embed_in, embed_ref, sems.at[0]),
        pltpu.make_async_copy(queue_in, queue_ref, sems.at[1]),
    ]
    for copy in fetch:
        copy.start()
    row, proto = row_ref[0], proto_ref[0]
    rows = embed_ref.shape[0]
    half = rows // 2
    images = half // CROPS
    local = image_ref[...] - row * (rows // CROPS)
    across = jnp.broadcast_to(local, (rows, rows)).astype(f32)
    down = jnp.transpose(across, (1, 0))
    first = lax.broadcasted_iota(jnp.int32, (rows, rows), 0)
    second = lax.broadcasted_iota(jnp.int32, (rows, rows), 1)
    earlier = jnp.where((across == down) & (first < second), 1.0, 0.0)
    rank = jnp.sum(earlier, axis=0, keepdims=True).astype(jnp.int32)
    upper = jnp.where(local >= images, 1, 0)
    position = upper * half + rank * images + (local - upper * images)
    order = (first == position).astype(f32).astype(bf16)
    order_ref[...] = order
    for copy in fetch:
        copy.wait()
    normed = unit_rows(embed_ref[...])[0].astype(bf16)
    sorted_ref[...] = jnp.dot(order, normed, preferred_element_type=f32)
    queued_ref[...] = unit_rows(queue_ref[...])[0]
    share = rows * unit_ref.shape[0] // (rows + queue_ref.shape[0])
    queue_share = unit_ref.shape[0] - share
    unit_ref[0:share, :] = sorted_ref[pl.ds(pl.multiple_of(proto * share, share), share), :].astype(bf16)
    unit_ref[share:, :] = queued_ref[
        pl.ds(pl.multiple_of(proto * queue_share, queue_share), queue_share), :
    ].astype(bf16)


def row_sums(column, total_batch, queue_blocks, mass_ref, out_ref, wide=None):
    head = wide or BLOCK // 4
    width = mass_ref.shape[1]
    step = 128
    factor = column[0:1]
    ones = jnp.ones((8, 128), bf16)

    def one(index, carry):
        start = pl.multiple_of(index * BLOCK, BLOCK)
        out_ref[0:1, pl.ds(start, head)] = sum_terms(dot_nt(column, mass_ref[pl.ds(start, head), :]))
        for rows in range(head, BLOCK, step):
            here = pl.ds(pl.multiple_of(start + rows, step), step)
            total = None
            for low in range(0, width, 256):
                pair = mass_ref[here, low : low + 128] * factor[:, low : low + 128]
                pair += mass_ref[here, low + 128 : low + 256] * factor[:, low + 128 : low + 256]
                total = pair.astype(f32) if total is None else total + pair.astype(f32)
            high = total.astype(bf16)
            low = (total - high.astype(f32)).astype(bf16)
            out_ref[0:1, here] = (dot_nt(ones, high) + dot_nt(ones, low))[0:1]
        return carry

    lax.fori_loop(0, total_batch // BLOCK + queue_blocks, one, 0)


def kept_places(total_rows, total_batch, feat, width):
    across = width // feat
    pieces = [
        (total_rows + feat * (1 + index // across), feat * (index % across), feat * index)
        for index in range(total_batch // feat)
    ]
    return total_rows, pieces


def live_blocks(fill):
    return lax.div(fill + (BLOCK - 1), BLOCK)


def make_kernel(offsets, share, total_batch, row_ref, proto_ref, fill_ref, *refs):
    *inputs, mass_out, sums_ref, side_ref, batch_ref, columns_ref, mass_ref, queue_ref, col_ref, sems, strip_sems, kept_sems, out_sems = refs
    *units, strips_ref = inputs
    row, proto = row_ref[0], proto_ref[0]
    fill = fill_ref[0]
    z_count, unit_rows_count, _ = units[0].shape
    queue_share = unit_rows_count - share
    proto_count = 1 + max(other for _, other in offsets)
    y_count = 1 + max(y for y, _ in offsets)
    strip_copies = []
    z_count, y_count, features, _ = strips_ref.shape
    for z in range(z_count):
        for y in range(y_count):
            first = pl.multiple_of((z * y_count + (lax.rem(row, y_count) ^ y)) * features, features)
            strip_copies.append(
                pltpu.make_async_copy(
                    strips_ref.at[z, y], columns_ref.at[pl.ds(first, features), :], strip_sems.at[z, y]
                )
            )
    for copy in strip_copies:
        copy.start()
    copies = []
    for index, (unit, (y, other)) in enumerate(zip(units, offsets)):
        for z in range(z_count):
            place = (row ^ (z * y_count + y)) * proto_count + (proto ^ other)
            crops = pl.multiple_of(place * share, share)
            queued = pl.multiple_of(place * queue_share, queue_share)
            copies.append(
                pltpu.make_async_copy(
                    unit.at[z, pl.ds(0, share), :],
                    batch_ref.at[pl.ds(crops, share), :],
                    sems.at[index, z, 0],
                )
            )
            copies.append(
                pltpu.make_async_copy(
                    unit.at[z, pl.ds(share, queue_share), :],
                    queue_ref.at[pl.ds(queued, queue_share), :],
                    sems.at[index, z, 1],
                )
            )
    for copy in copies[0::2] + copies[1::2]:
        copy.start()
    total_queue = queue_ref.shape[0]
    total_rows = total_batch + total_queue
    width = columns_ref.shape[1]
    col_ref[...] = jnp.zeros_like(col_ref)
    sums_ref[...] = jnp.zeros_like(sums_ref)
    ones = jnp.ones((8, 128), bf16)
    for copy in strip_copies:
        copy.wait()
    bound = jnp.max(jnp.abs(columns_ref[...].astype(f32)))
    side_ref[0:1, total_batch:] = jnp.full((1, 128), bound, f32)
    for copy in copies[0::2]:
        copy.wait()

    def add_columns(low, mass):
        col_ref[:, low : low + WIDE] += jnp.sum(mass.reshape(BLOCK // 8, 8, WIDE), axis=0)

    feat = columns_ref.shape[0]
    first, pieces = kept_places(total_rows, total_batch, feat, width)
    kept = [pltpu.make_async_copy(columns_ref, mass_out.at[pl.ds(first, feat), :], kept_sems.at[0])]
    for index, (place, lane, crop) in enumerate(pieces):
        kept.append(
            pltpu.make_async_copy(
                batch_ref.at[pl.ds(crop, feat), :],
                mass_out.at[pl.ds(place, feat), pl.ds(lane, feat)],
                kept_sems.at[1 + index],
            )
        )
    for copy in kept:
        copy.start()

    def keep(start):
        place = pl.ds(pl.multiple_of(start, BLOCK), BLOCK)
        return pltpu.make_async_copy(mass_ref.at[place, :], mass_out.at[place, :], out_sems)

    def crops_block(index, carry):
        start = pl.multiple_of(index * BLOCK, BLOCK)
        rows = batch_ref[pl.ds(start, BLOCK), :]
        lanes = None
        for low in range(0, width, WIDE):
            scores = jnp.dot(rows, columns_ref[:, low : low + WIDE], preferred_element_type=f32)
            soft = jnp.exp2(scores * SOFT_SCALE)
            mass = soft * soft
            mass_ref[pl.ds(start, BLOCK), low : low + WIDE] = mass.astype(bf16)
            add_columns(low, mass)
            for lane in range(0, WIDE, 128):
                part = soft[:, lane : lane + 128]
                lanes = part if lanes is None else lanes + part
        high, middle, small = bf16_terms(lanes)
        total = dot_nt(ones, high) + dot_nt(ones, middle) + dot_nt(ones, small)
        side_ref[0:1, pl.ds(start, BLOCK)] = total[0:1]
        keep(start).start()
        return carry

    lax.fori_loop(0, total_batch // BLOCK, crops_block, 0)

    for copy in copies[1::2]:
        copy.wait()

    def queue_block(index, masked):
        start = pl.multiple_of(index * BLOCK, BLOCK)
        rows = queue_ref[pl.ds(start, BLOCK), :]
        place = pl.ds(pl.multiple_of(total_batch + start, BLOCK), BLOCK)
        for low in range(0, width, WIDE):
            scores = jnp.dot(rows, columns_ref[:, low : low + WIDE], preferred_element_type=f32)
            soft = jnp.exp2(scores * SOFT_SCALE)
            mass = soft * soft
            if masked:
                live = lax.broadcasted_iota(jnp.int32, (BLOCK, WIDE), 0) < fill - start
                mass = jnp.where(live, mass, 0.0)
            mass_ref[place, low : low + WIDE] = mass.astype(bf16)
            add_columns(low, mass)
        keep(total_batch + start).start()

    def whole_block(index, carry):
        queue_block(index, False)
        return carry

    whole = lax.div(fill, BLOCK)
    lax.fori_loop(0, whole, whole_block, 0)

    @pl.when(live_blocks(fill) > whole)
    def _():
        queue_block(whole, True)

    column = term_rows(1.0 / jnp.sum(col_ref[...], axis=0, keepdims=True))
    row_sums(column, total_batch, live_blocks(fill), mass_ref, sums_ref)

    def finish(index, carry):
        keep(index * BLOCK).wait()
        return carry

    lax.fori_loop(0, total_batch // BLOCK + live_blocks(fill), finish, 0)
    for copy in kept:
        copy.wait()


def column_factor(fill, total_batch, parts, mass_ref, scale_ref, col_ref, spare_ref, make=None, ready=None):
    total_rows = scale_ref.shape[1]
    total = parts[0][0:1, 0:total_rows]
    for part in parts[1:]:
        total = total + part[0:1, 0:total_rows]
    place = lax.broadcasted_iota(jnp.int32, (1, total_rows), 1)
    scale = jnp.where(place < total_batch + fill, 1.0 / total, 0.0)
    scale_ref[...] = term_rows(scale)
    col_ref[...] = jnp.zeros_like(col_ref)
    spare_ref[...] = jnp.zeros_like(spare_ref)

    head = 3 * BLOCK // 4

    def add(index):
        start = pl.multiple_of(index * BLOCK, BLOCK)
        rows, rest = pl.ds(start, head), pl.ds(pl.multiple_of(start + head, 128), BLOCK - head)
        col_ref[...] += jnp.dot(scale_ref[:, rows], mass_ref[rows, :], preferred_element_type=f32)
        high, middle, low = (scale_ref[i : i + 1, rest].astype(f32) for i in range(3))
        factor = jnp.transpose(jnp.broadcast_to(high + middle + low, (128, BLOCK - head)), (1, 0))
        for low in range(0, mass_ref.shape[1], 128):
            part = mass_ref[rest, low : low + 128].astype(f32) * factor
            spare_ref[:, low : low + 128] += jnp.sum(part.reshape((BLOCK - head) // 8, 8, 128), axis=0)

    def crops(index, carry):
        if make is not None:
            make(index)
        add(index)
        return carry

    def queue(index, carry):
        if ready is not None:
            ready(index)
        add(total_batch // BLOCK + index)
        return carry

    lax.fori_loop(0, total_batch // BLOCK, crops, 0)
    lax.fori_loop(0, live_blocks(fill), queue, 0)
    return 1.0 / (sum_terms(col_ref[...]) + jnp.sum(spare_ref[...], axis=0, keepdims=True))


def sweep_kernel(total_batch, fill_ref, mass_in, *refs):
    *parts, sums_ref, mass_ref, scale_ref, col_ref, spare_ref, batch_ref, columns_ref, sems, kept_sems = refs
    fill = fill_ref[0]
    feat, width = columns_ref.shape
    first, pieces = kept_places(mass_ref.shape[0], total_batch, feat, width)
    kept = [pltpu.make_async_copy(mass_in.at[pl.ds(first, feat), :], columns_ref, kept_sems.at[0])]
    for index, (place, lane, crop) in enumerate(pieces):
        kept.append(
            pltpu.make_async_copy(
                mass_in.at[pl.ds(place, feat), pl.ds(lane, feat)],
                batch_ref.at[pl.ds(crop, feat), :],
                kept_sems.at[1 + index],
            )
        )
    for copy in kept:
        copy.start()

    def fetch(index):
        rows = pl.ds(pl.multiple_of(total_batch + index * BLOCK, BLOCK), BLOCK)
        return pltpu.make_async_copy(mass_in.at[rows, :], mass_ref.at[rows, :], sems.at[index])

    def start(index, carry):
        fetch(index).start()
        return carry

    lax.fori_loop(0, live_blocks(fill), start, 0)

    for copy in kept:
        copy.wait()

    def make(index):
        rows = pl.ds(pl.multiple_of(index * BLOCK, BLOCK), BLOCK)
        crops = batch_ref[rows, :]
        for low in range(0, width, WIDE):
            scores = jnp.dot(crops, columns_ref[:, low : low + WIDE], preferred_element_type=f32)
            soft = jnp.exp2(scores * SOFT_SCALE)
            mass_ref[rows, low : low + WIDE] = (soft * soft).astype(bf16)

    column = column_factor(
        fill, total_batch, parts, mass_ref, scale_ref, col_ref, spare_ref, make, lambda index: fetch(index).wait()
    )
    sums_ref[...] = jnp.zeros_like(sums_ref)
    row_sums(term_rows(column), total_batch, live_blocks(fill), mass_ref, sums_ref)


def last_kernel(total_batch, fill_ref, side_ref, mass_ref, *refs):
    *parts, sums_ref, column_ref, scale_ref, col_ref, spare_ref = refs
    fill = fill_ref[0]
    column = column_factor(fill, total_batch, parts, mass_ref, scale_ref, col_ref, spare_ref)
    column_ref[...] = column
    sums_ref[0:1, total_batch:] = side_ref[...]
    row_sums(term_rows(column), total_batch, 0, mass_ref, sums_ref, BLOCK)


def slope_kernel(crop_count, first, last, batch_ref, columns_ref, column_ref, *refs):
    *parts, normed_out, grad_ref, loss_ref, back_ref, normed_ref, sems = refs
    total_batch, width = batch_ref.shape[0], last - first
    rows = min(2 * ROWS, total_batch)
    wide = min(width, WIDE)
    grad_ref[...] = jnp.zeros_like(grad_ref)
    loss_ref[...] = jnp.zeros_like(loss_ref)

    bound = functools.reduce(jnp.add, [part[0:1, 2 * total_batch :] for part in parts])
    bound = 20.0 * bound + 1e-30
    back_ref[...] = jnp.broadcast_to(bound / 32768.0, (8, 128))
    scale = jnp.concatenate([32768.0 / bound] * (batch_ref.shape[1] // 128), axis=1)

    def keep(index):
        place = pl.ds(pl.multiple_of(index * rows, rows), rows)
        return pltpu.make_async_copy(normed_ref.at[place, :], normed_out.at[place, :], sems.at[index])

    def one(index, carry):
        start = pl.multiple_of(index * rows, rows)
        here = pl.ds(start, rows)

        later = pl.ds(pl.multiple_of(total_batch + start, rows), rows)
        code, soft_line = parts[0][0:1, here], parts[0][0:1, later]
        for part in parts[1:]:
            code, soft_line = code + part[0:1, here], soft_line + part[0:1, later]
        lines = [1.0 / ((crop_count - 1) * code), 10.0 / soft_line, jnp.log(soft_line)]
        factors = jnp.transpose(jnp.concatenate(lines + [jnp.zeros((125, rows), f32)], axis=0), (1, 0))
        code_factor, soft_factor, log_soft = (factors[:, i : i + 1] for i in range(3))
        crops = batch_ref[here, :]
        crops_t = jnp.transpose(crops.astype(f32), (1, 0)).astype(bf16)
        normed = jnp.zeros((rows, crops.shape[1]), f32)
        loss = jnp.zeros((8, 128), f32)
        for low in range(0, width, wide):
            place = slice(first + low, first + low + wide)
            columns = columns_ref[:, place]
            scores = jnp.dot(crops, columns, preferred_element_type=f32)
            soft = jnp.exp2(scores * SOFT_SCALE)
            assigned = (soft * soft) * column_ref[0:1, place] * code_factor
            slabs = assigned.reshape(rows // 128, crop_count, 128 // crop_count, wide)
            grouped = jnp.sum(slabs, axis=1, keepdims=True)
            targets = (grouped - slabs).reshape(rows, wide)
            logits = (soft * soft_factor - targets * 10.0).astype(bf16)
            terms = targets * (log_soft - scores * 10.0)
            folded = jnp.sum(terms.reshape(rows // 8, 8, wide), axis=0)
            for lane in range(0, wide, 128):
                loss = loss + folded[:, lane : lane + 128]
            grad_ref[:, low : low + wide] += jnp.dot(crops_t, logits, preferred_element_type=f32)
            normed = normed + dot_nt(logits, columns)
        normed_ref[here, :] = normed * scale
        keep(index).start()
        loss_ref[...] += loss
        return carry

    lax.fori_loop(0, total_batch // rows, one, 0)

    loss = jnp.maximum(jnp.sum(loss_ref[...]), 1e-30)
    exponent = jnp.floor(jnp.log2(jnp.full((1, 128), loss, f32)))
    mantissa = loss / jnp.exp2(exponent)
    high = jnp.floor(mantissa * 1024.0) / 1024.0
    lane = lax.broadcasted_iota(jnp.int32, (1, 128), 1)
    loss_ref[...] = jnp.broadcast_to(
        jnp.where(lane == 0, exponent, jnp.where(lane == 1, high, (mantissa - high) * 2048.0)), (8, 128)
    )

    def kept(index, carry):
        keep(index).wait()
        return carry

    lax.fori_loop(0, total_batch // rows, kept, 0)


def finish_kernel(piece_count, proto_ref, embed_ref, order_ref, back_ref, *refs):
    *pieces, out_ref, loss_ref, sorted_ref = refs
    rows = embed_ref.shape[0]
    size = rows // piece_count
    proto = proto_ref[0]
    for index, piece in enumerate(pieces):
        other = proto ^ index
        place = (other % 2) * (piece_count // 2) + other // 2
        sorted_ref[pl.ds(pl.multiple_of(place * size, size), size), :] = piece[0:size, :]
    loss_ref[0] = jnp.max(functools.reduce(jnp.add, [piece[size:, 0:128] for piece in pieces]))
    order = order_ref[...]
    high, middle, low = bf16_terms(sorted_ref[...])
    grad = dot_tn(order, high) + dot_tn(order, middle) + dot_tn(order, low)
    grad = grad * back_ref[0:1, 0:1]
    exact, inverse = unit_rows(embed_ref[...])
    out_ref[...] = inverse * (grad - exact * jnp.sum(exact * grad, axis=1, keepdims=True))


def solution(mesh):
    row_count, proto_count = mesh.shape["row"], mesh.shape["proto"]
    z_count = min(4, row_count)
    y_count = row_count // z_count
    x_count = proto_count // 2

    def shift_row(values, z, y):
        offset = z * y_count + y
        return lax.ppermute(values, "row", [(i, i ^ offset) for i in range(row_count)])

    def shift_proto(values, offset):
        return lax.ppermute(values, "proto", [(i, i ^ offset) for i in range(proto_count)])

    def shift_xy(values, x, y):
        pairs = []
        for i in range(row_count):
            for j in range(proto_count):
                pairs.append((i * proto_count + j, (i ^ y) * proto_count + (j ^ (2 * x))))
        return lax.ppermute(values, ("row", "proto"), pairs)

    def all_sum_parts(values):
        values = values + shift_proto(values, 1)
        moved = [shift_xy(values, x, y) for y in range(y_count) for x in range(x_count) if x or y]
        values = functools.reduce(jnp.add, moved, values)
        return [values] + [shift_row(values, z, 0) for z in range(1, z_count)]

    def body(embeddings, queue_feats, prototypes, crop_image, fill_count):
        batch_rows, feat = embeddings.shape
        queue_rows = queue_feats.shape[0]
        share, queue_share = batch_rows // proto_count, queue_rows // proto_count
        half = batch_rows // 2
        total_batch, total_queue = batch_rows * row_count, queue_rows * row_count
        total_rows = total_batch + total_queue
        row, proto = lax.axis_index("row"), lax.axis_index("proto")
        core, x, y, z = proto % 2, proto // 2, row % y_count, row // y_count
        places = [row.reshape(1).astype(jnp.int32), proto.reshape(1).astype(jnp.int32)]
        unit_rows_count = share + queue_share

        def pick(values, index, axis):
            return lax.dynamic_index_in_dim(values, index, axis, keepdims=False)

        unit, order = pl.pallas_call(
            prep_kernel,
            name="prep",
            out_shape=[
                jax.ShapeDtypeStruct((unit_rows_count, feat), bf16),
                jax.ShapeDtypeStruct((batch_rows, batch_rows), bf16),
            ],
            in_specs=[SMEM, SMEM, VMEM, ANY, ANY],
            out_specs=[VMEM, VMEM],
            scratch_shapes=[
                pltpu.VMEM((batch_rows, feat), bf16),
                pltpu.VMEM((queue_rows, feat), bf16),
                pltpu.VMEM((batch_rows, feat), f32),
                pltpu.VMEM((queue_rows, feat), f32),
                pltpu.SemaphoreType.DMA((2,)),
            ],
            compiler_params=limit(56),
        )(*places, crop_image.reshape(1, batch_rows), embeddings, queue_feats)

        lines = [unit] + [shift_row(unit, z, 0) for z in range(1, z_count)]
        width = prototypes.shape[1] // row_count
        features = prototypes.shape[0]

        def strip(dy):
            places = [((other * y_count) + (y ^ dy)) * width for other in range(z_count)]
            return jnp.stack([lax.dynamic_slice(prototypes, (0, place), (features, width)) for place in places])

        strips = [shift_row(strip(dy), 0, dy) if dy else strip(dy) for dy in range(y_count)]
        lanes = [[other * y_count + own for other in range(z_count)] for own in range(y_count)]
        *lines, strips = lax.optimization_barrier((*lines, jnp.stack(strips, axis=1)))
        lines = jnp.stack(lines)
        strips = lax.all_to_all(
            strips, "row", split_axis=0, concat_axis=0, axis_index_groups=lanes, tiled=True
        )

        offsets, units = [], []
        for dy in range(y_count):
            there = shift_row(lines, 0, dy) if dy else lines
            for dx in range(x_count):
                moved = shift_proto(there, 2 * dx) if dx else there
                offsets += [(dy, 2 * dx), (dy, 2 * dx + 1)]
                units += [moved, shift_proto(moved, 1)]

        mass, sums, side, batch, columns = pl.pallas_call(
            functools.partial(make_kernel, offsets, share, total_batch),
            name="make_mass",
            out_shape=[
                jax.ShapeDtypeStruct((total_rows + feat * (1 + total_batch // width), width), bf16),
                jax.ShapeDtypeStruct((1, total_rows), f32),
                jax.ShapeDtypeStruct((1, total_batch + 128), f32),
                jax.ShapeDtypeStruct((total_batch, feat), bf16),
                jax.ShapeDtypeStruct((feat, width), bf16),
            ],
            in_specs=[SMEM, SMEM, SMEM] + [ANY] * (len(units) + 1),
            out_specs=[ANY, VMEM, VMEM, VMEM, VMEM],
            scratch_shapes=[
                pltpu.VMEM((total_rows, width), bf16),
                pltpu.VMEM((total_queue, feat), bf16),
                pltpu.VMEM((8, width), f32),
                pltpu.SemaphoreType.DMA((len(units), z_count, 2)),
                pltpu.SemaphoreType.DMA((z_count, y_count)),
                pltpu.SemaphoreType.DMA((1 + total_batch // feat,)),
                pltpu.SemaphoreType.DMA,
            ],
            compiler_params=limit(53),
        )(*places, fill_count, *units, strips)

        vectors = [pltpu.VMEM((8, total_rows), bf16), pltpu.VMEM((8, width), f32), pltpu.VMEM((8, width), f32)]
        sums = pl.pallas_call(
            functools.partial(sweep_kernel, total_batch),
            name="sweep",
            out_shape=jax.ShapeDtypeStruct((1, total_rows), f32),
            in_specs=[SMEM, ANY] + [VMEM] * z_count,
            out_specs=VMEM,
            scratch_shapes=[pltpu.VMEM((total_rows, width), bf16)]
            + vectors
            + [
                pltpu.VMEM((total_batch, feat), bf16),
                pltpu.VMEM((feat, width), bf16),
                pltpu.SemaphoreType.DMA((total_queue // BLOCK,)),
                pltpu.SemaphoreType.DMA((1 + total_batch // feat,)),
            ],
            compiler_params=limit(33),
        )(fill_count, mass, *all_sum_parts(sums))

        code_sums, column = pl.pallas_call(
            functools.partial(last_kernel, total_batch),
            name="last_sweep",
            out_shape=[
                jax.ShapeDtypeStruct((1, 2 * total_batch + 128), f32),
                jax.ShapeDtypeStruct((1, width), f32),
            ],
            in_specs=[SMEM] + [VMEM] * (2 + z_count),
            out_specs=[VMEM, VMEM],
            scratch_shapes=vectors,
            compiler_params=limit(8),
        )(fill_count, side, mass, *all_sum_parts(sums))

        code_parts = all_sum_parts(code_sums)

        def slopes(first, last, batch):
            return pl.pallas_call(
                functools.partial(slope_kernel, CROPS, first, last),
                name="slopes",
                out_shape=[
                    jax.ShapeDtypeStruct((total_batch, feat), f32),
                    jax.ShapeDtypeStruct((feat, last - first), f32),
                    jax.ShapeDtypeStruct((8, 128), f32),
                    jax.ShapeDtypeStruct((8, 128), f32),
                ],
                in_specs=[VMEM] * (3 + z_count),
                out_specs=[ANY, VMEM, VMEM, VMEM],
                scratch_shapes=[
                    pltpu.VMEM((total_batch, feat), f32),
                    pltpu.SemaphoreType.DMA((total_batch // ROWS,)),
                ],
                compiler_params=limit(24),
            )(batch, columns, column, *code_parts)

        def as_blocks(grad_columns):
            return grad_columns.astype(f16).reshape(row_count, feat // row_count, -1)

        def exchange(blocks):
            return lax.all_to_all(blocks, "row", split_axis=0, concat_axis=0, tiled=True)

        normed_part, grad_columns, loss, back = slopes(0, width, batch)
        size = half // x_count

        pieces = normed_part.reshape(z_count, y_count, 2, x_count, size, feat)

        away = shift_proto(pick(pieces, 1 - core, 2).astype(f16), 1)
        kept = pick(pieces, core, 2) + away.astype(f32)
        total = None
        for dy in range(y_count):
            for dx in range(x_count):
                part = pick(pick(kept, x ^ dx, 2), y ^ dy, 1)
                if dx or dy:
                    part = shift_xy(part.astype(f16), dx, dy).astype(f32)
                total = part if total is None else total + part
        arriving = [shift_row(pick(total, z ^ dz, 0).astype(f16), dz, 0) for dz in range(1, z_count)]

        sent = jnp.concatenate([as_blocks(grad_columns), jnp.broadcast_to(loss[0:1].astype(f16), (row_count, feat // row_count, 128))], axis=2)
        got = exchange(sent)
        grad_proto = got[:, :, :width].astype(f32)
        grad_proto = grad_proto.transpose(1, 0, 2).reshape(feat // row_count, row_count * width)
        code = got[:, 0, width:].astype(f32)
        losses = jnp.sum((code[:, 1] + code[:, 2] / 2048.0) * jnp.exp2(code[:, 0])) / total_batch
        *arriving, losses = lax.optimization_barrier((*arriving, losses))
        piece = functools.reduce(jnp.add, [part.astype(f32) for part in arriving], pick(total, z, 0))
        piece = jnp.concatenate([piece, jnp.full((8, feat), losses, f32)], axis=0)

        gathered = [piece] + [shift_proto(piece, k) for k in range(1, proto_count)]
        grad_embed, loss = pl.pallas_call(
            functools.partial(finish_kernel, proto_count),
            name="finish",
            out_shape=[
                jax.ShapeDtypeStruct((batch_rows, feat), f32),
                jax.ShapeDtypeStruct((1,), f32),
            ],
            in_specs=[SMEM] + [VMEM] * (3 + proto_count),
            out_specs=[VMEM, SMEM],
            scratch_shapes=[pltpu.VMEM((batch_rows, feat), f32)],
            compiler_params=limit(8),
        )(proto.reshape(1).astype(jnp.int32), embeddings, order, back, *gathered)
        return grad_embed, grad_proto, loss

    placed = (P("row", None), P("row", None), P("row", "proto"), P("row"), P())
    return jax.shard_map(
        body,
        mesh=mesh,
        in_specs=placed,
        out_specs=(P("row", None), P("row", "proto"), P()),
        check_vma=False,
    )
```

```python
import functools

import jax
import jax.numpy as jnp
from jax import lax
from jax.experimental import pallas as pl
from jax.experimental.pallas import tpu as pltpu
from jax.sharding import PartitionSpec as P

CROPS = 8
LOG2E = 1.4426950408889634
SOFT_SCALE = 10.0 * LOG2E
BLOCK = 1024
WIDE = 256
ROWS = 1024

f32 = jnp.float32
bf16 = jnp.bfloat16
f16 = jnp.float16

VMEM = pl.BlockSpec(memory_space=pltpu.VMEM)
SMEM = pl.BlockSpec(memory_space=pltpu.SMEM)
ANY = pl.BlockSpec(memory_space=pl.ANY)


def limit(mib):
    return pltpu.CompilerParams(vmem_limit_bytes=mib << 20)


def bf16_terms(values):
    high = values.astype(bf16)
    rest = values - high.astype(f32)
    middle = rest.astype(bf16)
    return high, middle, (rest - middle.astype(f32)).astype(bf16)


def term_rows(values):
    high, middle, low = bf16_terms(values)
    return jnp.concatenate([high, middle, low] + [jnp.zeros_like(high)] * 5, axis=0)


def sum_terms(products):
    return products[0:1] + products[1:2] + products[2:3]


def dot_nt(left, right):
    return lax.dot_general(left, right, (((1,), (1,)), ((), ())), preferred_element_type=f32)


def dot_tn(left, right):
    return lax.dot_general(left, right, (((0,), (0,)), ((), ())), preferred_element_type=f32)


def unit_rows(raw):
    values = raw.astype(f32)
    inverse = lax.rsqrt(jnp.sum(values * values, axis=1, keepdims=True) + 1e-06)
    return values * inverse, inverse


def prep_kernel(
    row_ref, proto_ref, image_ref, embed_in, queue_in, unit_ref, order_ref, embed_ref, queue_ref, sorted_ref, queued_ref, sems
):
    fetch = [
        pltpu.make_async_copy(embed_in, embed_ref, sems.at[0]),
        pltpu.make_async_copy(queue_in, queue_ref, sems.at[1]),
    ]
    for copy in fetch:
        copy.start()
    row, proto = row_ref[0], proto_ref[0]
    rows = embed_ref.shape[0]
    half = rows // 2
    images = half // CROPS
    local = image_ref[...] - row * (rows // CROPS)
    across = jnp.broadcast_to(local, (rows, rows)).astype(f32)
    down = jnp.transpose(across, (1, 0))
    first = lax.broadcasted_iota(jnp.int32, (rows, rows), 0)
    second = lax.broadcasted_iota(jnp.int32, (rows, rows), 1)
    earlier = jnp.where((across == down) & (first < second), 1.0, 0.0)
    rank = jnp.sum(earlier, axis=0, keepdims=True).astype(jnp.int32)
    upper = jnp.where(local >= images, 1, 0)
    position = upper * half + rank * images + (local - upper * images)
    order = (first == position).astype(f32).astype(bf16)
    order_ref[...] = order
    for copy in fetch:
        copy.wait()
    normed = unit_rows(embed_ref[...])[0].astype(bf16)
    sorted_ref[...] = jnp.dot(order, normed, preferred_element_type=f32)
    queued_ref[...] = unit_rows(queue_ref[...])[0]
    share = rows * unit_ref.shape[0] // (rows + queue_ref.shape[0])
    queue_share = unit_ref.shape[0] - share
    unit_ref[0:share, :] = sorted_ref[pl.ds(pl.multiple_of(proto * share, share), share), :].astype(bf16)
    unit_ref[share:, :] = queued_ref[
        pl.ds(pl.multiple_of(proto * queue_share, queue_share), queue_share), :
    ].astype(bf16)


def row_sums(column, total_batch, fill, mass_ref, out_ref, exact=False):
    width = mass_ref.shape[1]
    step = 128
    factor = column[0:1]
    ones = jnp.ones((8, 128), bf16)

    def one(start, size):
        head = size if exact else size // 4
        out_ref[0:1, pl.ds(start, head)] = sum_terms(dot_nt(column, mass_ref[pl.ds(start, head), :]))
        for rows in range(head, size, step):
            here = pl.ds(pl.multiple_of(start + rows, step), step)
            total = None
            for low in range(0, width, 256):
                pair = mass_ref[here, low : low + 128] * factor[:, low : low + 128]
                pair += mass_ref[here, low + 128 : low + 256] * factor[:, low + 128 : low + 256]
                total = pair.astype(f32) if total is None else total + pair.astype(f32)
            high = total.astype(bf16)
            low = (total - high.astype(f32)).astype(bf16)
            out_ref[0:1, here] = (dot_nt(ones, high) + dot_nt(ones, low))[0:1]

    def queue(start, size, cut):
        one(pl.multiple_of(total_batch + start, BLOCK), size)

    each_block(total_batch, fill, one, None if fill is None else queue)


def kept_places(total_rows, total_batch, feat, width):
    across = width // feat
    pieces = [
        (total_rows + feat * (1 + index // across), feat * (index % across), feat * index)
        for index in range(total_batch // feat)
    ]
    return total_rows, pieces


def each_block(total_batch, fill, crops_body, queue_body):
    def crops(index, carry):
        crops_body(pl.multiple_of(index * BLOCK, BLOCK), BLOCK)
        return carry

    def queue(index, carry):
        queue_body(pl.multiple_of(index * BLOCK, BLOCK), BLOCK, False)
        return carry

    if crops_body is not None:
        lax.fori_loop(0, total_batch // BLOCK, crops, 0)
    if queue_body is not None:
        whole = lax.div(fill, BLOCK)
        rest = fill - whole * BLOCK
        lax.fori_loop(0, whole, queue, 0)
        start = pl.multiple_of(whole * BLOCK, BLOCK)

        @pl.when(rest > BLOCK // 2)
        def _():
            queue_body(start, BLOCK, True)

        @pl.when((rest > 0) & (rest <= BLOCK // 2))
        def _():
            queue_body(start, BLOCK // 2, True)


def make_kernel(offsets, share, total_batch, row_ref, proto_ref, fill_ref, *refs):
    *inputs, mass_out, sums_ref, side_ref, batch_ref, columns_ref, mass_ref, queue_ref, col_ref, sems, strip_sems, kept_sems, out_sems = refs
    *units, strips_ref = inputs
    row, proto = row_ref[0], proto_ref[0]
    fill = fill_ref[0]
    z_count, unit_rows_count, _ = units[0].shape
    queue_share = unit_rows_count - share
    proto_count = 1 + max(other for _, other in offsets)
    y_count = 1 + max(y for y, _ in offsets)
    strip_copies = []
    z_count, y_count, features, _ = strips_ref.shape
    for z in range(z_count):
        for y in range(y_count):
            first = pl.multiple_of((z * y_count + (lax.rem(row, y_count) ^ y)) * features, features)
            strip_copies.append(
                pltpu.make_async_copy(
                    strips_ref.at[z, y], columns_ref.at[pl.ds(first, features), :], strip_sems.at[z, y]
                )
            )
    for copy in strip_copies:
        copy.start()
    copies = []
    for index, (unit, (y, other)) in enumerate(zip(units, offsets)):
        for z in range(z_count):
            place = (row ^ (z * y_count + y)) * proto_count + (proto ^ other)
            crops = pl.multiple_of(place * share, share)
            queued = pl.multiple_of(place * queue_share, queue_share)
            copies.append(
                pltpu.make_async_copy(
                    unit.at[z, pl.ds(0, share), :],
                    batch_ref.at[pl.ds(crops, share), :],
                    sems.at[index, z, 0],
                )
            )
            copies.append(
                pltpu.make_async_copy(
                    unit.at[z, pl.ds(share, queue_share), :],
                    queue_ref.at[pl.ds(queued, queue_share), :],
                    sems.at[index, z, 1],
                )
            )
    for copy in copies[0::2] + copies[1::2]:
        copy.start()
    total_queue = queue_ref.shape[0]
    total_rows = total_batch + total_queue
    width = columns_ref.shape[1]
    col_ref[...] = jnp.zeros_like(col_ref)
    sums_ref[...] = jnp.zeros_like(sums_ref)
    ones = jnp.ones((8, 128), bf16)
    for copy in strip_copies:
        copy.wait()
    bound = jnp.max(jnp.abs(columns_ref[...].astype(f32)))
    side_ref[0:1, total_batch:] = jnp.full((1, 128), bound, f32)
    for copy in copies[0::2]:
        copy.wait()

    def add_columns(low, mass):
        col_ref[:, low : low + WIDE] += jnp.sum(mass.reshape(mass.shape[0] // 8, 8, WIDE), axis=0)

    feat = columns_ref.shape[0]
    first, pieces = kept_places(total_rows, total_batch, feat, width)
    kept = [pltpu.make_async_copy(columns_ref, mass_out.at[pl.ds(first, feat), :], kept_sems.at[0])]
    for index, (place, lane, crop) in enumerate(pieces):
        kept.append(
            pltpu.make_async_copy(
                batch_ref.at[pl.ds(crop, feat), :],
                mass_out.at[pl.ds(place, feat), pl.ds(lane, feat)],
                kept_sems.at[1 + index],
            )
        )
    for copy in kept:
        copy.start()

    def keep(start, size):
        place = pl.ds(pl.multiple_of(start, BLOCK), size)
        return pltpu.make_async_copy(mass_ref.at[place, :], mass_out.at[place, :], out_sems)

    def crops_block(start, size):
        rows = batch_ref[pl.ds(start, BLOCK), :]
        lanes = None
        for low in range(0, width, WIDE):
            scores = jnp.dot(rows, columns_ref[:, low : low + WIDE], preferred_element_type=f32)
            soft = jnp.exp2(scores * SOFT_SCALE)
            mass = soft * soft
            mass_ref[pl.ds(start, BLOCK), low : low + WIDE] = mass.astype(bf16)
            add_columns(low, mass)
            for lane in range(0, WIDE, 128):
                part = soft[:, lane : lane + 128]
                lanes = part if lanes is None else lanes + part
        high, middle, small = bf16_terms(lanes)
        total = dot_nt(ones, high) + dot_nt(ones, middle) + dot_nt(ones, small)
        side_ref[0:1, pl.ds(start, BLOCK)] = total[0:1]
        keep(start, size).start()

    each_block(total_batch, fill, crops_block, None)

    for copy in copies[1::2]:
        copy.wait()

    def queue_block(start, size, cut):
        rows = queue_ref[pl.ds(start, size), :]
        place = pl.ds(pl.multiple_of(total_batch + start, BLOCK), size)
        for low in range(0, width, WIDE):
            scores = jnp.dot(rows, columns_ref[:, low : low + WIDE], preferred_element_type=f32)
            soft = jnp.exp2(scores * SOFT_SCALE)
            mass = soft * soft
            if cut:
                live = lax.broadcasted_iota(jnp.int32, (size, WIDE), 0) < fill - start
                mass = jnp.where(live, mass, 0.0)
            mass_ref[place, low : low + WIDE] = mass.astype(bf16)
            add_columns(low, mass)
        keep(total_batch + start, size).start()

    each_block(total_batch, fill, None, queue_block)
    column = term_rows(1.0 / jnp.sum(col_ref[...], axis=0, keepdims=True))
    row_sums(column, total_batch, fill, mass_ref, sums_ref)
    each_block(
        total_batch,
        fill,
        lambda start, size: keep(start, size).wait(),
        lambda start, size, cut: keep(total_batch + start, size).wait(),
    )
    for copy in kept:
        copy.wait()


def column_factor(fill, total_batch, parts, mass_ref, scale_ref, col_ref, spare_ref, settle=None, make=None, ready=None):
    total_rows = scale_ref.shape[1]
    total = parts[0][0:1, 0:total_rows]
    for part in parts[1:]:
        total = total + part[0:1, 0:total_rows]
    place = lax.broadcasted_iota(jnp.int32, (1, total_rows), 1)
    scale = jnp.where(place < total_batch + fill, 1.0 / total, 0.0)
    scale_ref[...] = term_rows(scale)
    col_ref[...] = jnp.zeros_like(col_ref)
    spare_ref[...] = jnp.zeros_like(spare_ref)

    def add(start, size):
        head = 3 * size // 4
        rows, rest = pl.ds(start, head), pl.ds(pl.multiple_of(start + head, 128), size - head)
        col_ref[...] += jnp.dot(scale_ref[:, rows], mass_ref[rows, :], preferred_element_type=f32)
        high, middle, low = (scale_ref[i : i + 1, rest].astype(f32) for i in range(3))
        factor = jnp.transpose(jnp.broadcast_to(high + middle + low, (128, size - head)), (1, 0))
        for low in range(0, mass_ref.shape[1], 128):
            part = mass_ref[rest, low : low + 128].astype(f32) * factor
            spare_ref[:, low : low + 128] += jnp.sum(part.reshape((size - head) // 8, 8, 128), axis=0)

    def crops(start, size):
        if make is not None:
            make(start, size)
        add(start, size)

    def queue(start, size, cut):
        if ready is not None:
            ready(start, size)
        add(pl.multiple_of(total_batch + start, BLOCK), size)

    if settle is not None:
        settle()
    each_block(total_batch, fill, crops, queue)
    return 1.0 / (sum_terms(col_ref[...]) + jnp.sum(spare_ref[...], axis=0, keepdims=True))


def sweep_kernel(total_batch, fill_ref, mass_in, *refs):
    *parts, sums_ref, mass_ref, scale_ref, col_ref, spare_ref, batch_ref, columns_ref, sems, kept_sems = refs
    fill = fill_ref[0]
    feat, width = columns_ref.shape
    first, pieces = kept_places(mass_ref.shape[0], total_batch, feat, width)
    kept = [pltpu.make_async_copy(mass_in.at[pl.ds(first, feat), :], columns_ref, kept_sems.at[0])]
    for index, (place, lane, crop) in enumerate(pieces):
        kept.append(
            pltpu.make_async_copy(
                mass_in.at[pl.ds(place, feat), pl.ds(lane, feat)],
                batch_ref.at[pl.ds(crop, feat), :],
                kept_sems.at[1 + index],
            )
        )
    for copy in kept:
        copy.start()

    def fetch(start, size):
        rows = pl.ds(pl.multiple_of(total_batch + start, BLOCK), size)
        return pltpu.make_async_copy(mass_in.at[rows, :], mass_ref.at[rows, :], sems.at[lax.div(start, BLOCK)])

    each_block(total_batch, fill, None, lambda start, size, cut: fetch(start, size).start())

    def settle():
        for copy in kept:
            copy.wait()

    def make(start, size):
        rows = pl.ds(start, size)
        crops = batch_ref[rows, :]
        for low in range(0, width, WIDE):
            scores = jnp.dot(crops, columns_ref[:, low : low + WIDE], preferred_element_type=f32)
            soft = jnp.exp2(scores * SOFT_SCALE)
            mass_ref[rows, low : low + WIDE] = (soft * soft).astype(bf16)

    column = column_factor(
        fill,
        total_batch,
        parts,
        mass_ref,
        scale_ref,
        col_ref,
        spare_ref,
        settle,
        make,
        lambda start, size: fetch(start, size).wait(),
    )
    sums_ref[...] = jnp.zeros_like(sums_ref)
    row_sums(term_rows(column), total_batch, fill, mass_ref, sums_ref)


def last_kernel(total_batch, fill_ref, side_ref, mass_ref, *refs):
    *parts, sums_ref, column_ref, scale_ref, col_ref, spare_ref = refs
    fill = fill_ref[0]
    column = column_factor(fill, total_batch, parts, mass_ref, scale_ref, col_ref, spare_ref)
    column_ref[...] = column
    sums_ref[0:1, total_batch:] = side_ref[...]
    row_sums(term_rows(column), total_batch, None, mass_ref, sums_ref, True)


def slope_kernel(crop_count, first, last, batch_ref, columns_ref, column_ref, *refs):
    *parts, normed_out, grad_ref, loss_ref, back_ref, normed_ref, sems = refs
    total_batch, width = batch_ref.shape[0], last - first
    rows = min(2 * ROWS, total_batch)
    wide = min(width, WIDE)
    grad_ref[...] = jnp.zeros_like(grad_ref)
    loss_ref[...] = jnp.zeros_like(loss_ref)

    bound = functools.reduce(jnp.add, [part[0:1, 2 * total_batch :] for part in parts])
    bound = 20.0 * bound + 1e-30
    back_ref[...] = jnp.broadcast_to(bound / 32768.0, (8, 128))
    scale = jnp.concatenate([32768.0 / bound] * (batch_ref.shape[1] // 128), axis=1)

    def keep(index):
        place = pl.ds(pl.multiple_of(index * rows, rows), rows)
        return pltpu.make_async_copy(normed_ref.at[place, :], normed_out.at[place, :], sems.at[index])

    def one(index, carry):
        start = pl.multiple_of(index * rows, rows)
        here = pl.ds(start, rows)

        later = pl.ds(pl.multiple_of(total_batch + start, rows), rows)
        code, soft_line = parts[0][0:1, here], parts[0][0:1, later]
        for part in parts[1:]:
            code, soft_line = code + part[0:1, here], soft_line + part[0:1, later]
        lines = [1.0 / ((crop_count - 1) * code), 10.0 / soft_line, jnp.log(soft_line)]
        factors = jnp.transpose(jnp.concatenate(lines + [jnp.zeros((125, rows), f32)], axis=0), (1, 0))
        code_factor, soft_factor, log_soft = (factors[:, i : i + 1] for i in range(3))
        crops = batch_ref[here, :]
        crops_t = jnp.transpose(crops.astype(f32), (1, 0)).astype(bf16)
        normed = jnp.zeros((rows, crops.shape[1]), f32)
        loss = jnp.zeros((8, 128), f32)
        for low in range(0, width, wide):
            place = slice(first + low, first + low + wide)
            columns = columns_ref[:, place]
            scores = jnp.dot(crops, columns, preferred_element_type=f32)
            soft = jnp.exp2(scores * SOFT_SCALE)
            assigned = (soft * soft) * column_ref[0:1, place] * code_factor
            slabs = assigned.reshape(rows // 128, crop_count, 128 // crop_count, wide)
            grouped = jnp.sum(slabs, axis=1, keepdims=True)
            targets = (grouped - slabs).reshape(rows, wide)
            logits = (soft * soft_factor - targets * 10.0).astype(bf16)
            terms = targets * (log_soft - scores * 10.0)
            folded = jnp.sum(terms.reshape(rows // 8, 8, wide), axis=0)
            for lane in range(0, wide, 128):
                loss = loss + folded[:, lane : lane + 128]
            grad_ref[:, low : low + wide] += jnp.dot(crops_t, logits, preferred_element_type=f32)
            normed = normed + dot_nt(logits, columns)
        normed_ref[here, :] = normed * scale
        keep(index).start()
        loss_ref[...] += loss
        return carry

    lax.fori_loop(0, total_batch // rows, one, 0)

    loss = jnp.maximum(jnp.sum(loss_ref[...]), 1e-30)
    exponent = jnp.floor(jnp.log2(jnp.full((1, 128), loss, f32)))
    mantissa = loss / jnp.exp2(exponent)
    high = jnp.floor(mantissa * 1024.0) / 1024.0
    lane = lax.broadcasted_iota(jnp.int32, (1, 128), 1)
    loss_ref[...] = jnp.broadcast_to(
        jnp.where(lane == 0, exponent, jnp.where(lane == 1, high, (mantissa - high) * 2048.0)), (8, 128)
    )

    def kept(index, carry):
        keep(index).wait()
        return carry

    lax.fori_loop(0, total_batch // rows, kept, 0)


def finish_kernel(piece_count, proto_ref, embed_ref, order_ref, back_ref, *refs):
    *pieces, out_ref, loss_ref, sorted_ref = refs
    rows = embed_ref.shape[0]
    size = rows // piece_count
    proto = proto_ref[0]
    for index, piece in enumerate(pieces):
        other = proto ^ index
        place = (other % 2) * (piece_count // 2) + other // 2
        sorted_ref[pl.ds(pl.multiple_of(place * size, size), size), :] = piece[0:size, :]
    loss_ref[0] = jnp.max(functools.reduce(jnp.add, [piece[size:, 0:128] for piece in pieces]))
    order = order_ref[...]
    high, middle, low = bf16_terms(sorted_ref[...])
    grad = dot_tn(order, high) + dot_tn(order, middle) + dot_tn(order, low)
    grad = grad * back_ref[0:1, 0:1]
    exact, inverse = unit_rows(embed_ref[...])
    out_ref[...] = inverse * (grad - exact * jnp.sum(exact * grad, axis=1, keepdims=True))


def solution(mesh):
    row_count, proto_count = mesh.shape["row"], mesh.shape["proto"]
    z_count = min(4, row_count)
    y_count = row_count // z_count
    x_count = proto_count // 2

    def shift_row(values, z, y):
        offset = z * y_count + y
        return lax.ppermute(values, "row", [(i, i ^ offset) for i in range(row_count)])

    def shift_proto(values, offset):
        return lax.ppermute(values, "proto", [(i, i ^ offset) for i in range(proto_count)])

    def shift_xy(values, x, y):
        pairs = []
        for i in range(row_count):
            for j in range(proto_count):
                pairs.append((i * proto_count + j, (i ^ y) * proto_count + (j ^ (2 * x))))
        return lax.ppermute(values, ("row", "proto"), pairs)

    def all_sum_parts(values):
        values = values + shift_proto(values, 1)
        moved = [shift_xy(values, x, y) for y in range(y_count) for x in range(x_count) if x or y]
        values = functools.reduce(jnp.add, moved, values)
        return [values] + [shift_row(values, z, 0) for z in range(1, z_count)]

    def body(embeddings, queue_feats, prototypes, crop_image, fill_count):
        batch_rows, feat = embeddings.shape
        queue_rows = queue_feats.shape[0]
        share, queue_share = batch_rows // proto_count, queue_rows // proto_count
        half = batch_rows // 2
        total_batch, total_queue = batch_rows * row_count, queue_rows * row_count
        total_rows = total_batch + total_queue
        row, proto = lax.axis_index("row"), lax.axis_index("proto")
        core, x, y, z = proto % 2, proto // 2, row % y_count, row // y_count
        places = [row.reshape(1).astype(jnp.int32), proto.reshape(1).astype(jnp.int32)]
        unit_rows_count = share + queue_share

        def pick(values, index, axis):
            return lax.dynamic_index_in_dim(values, index, axis, keepdims=False)

        unit, order = pl.pallas_call(
            prep_kernel,
            name="prep",
            out_shape=[
                jax.ShapeDtypeStruct((unit_rows_count, feat), bf16),
                jax.ShapeDtypeStruct((batch_rows, batch_rows), bf16),
            ],
            in_specs=[SMEM, SMEM, VMEM, ANY, ANY],
            out_specs=[VMEM, VMEM],
            scratch_shapes=[
                pltpu.VMEM((batch_rows, feat), bf16),
                pltpu.VMEM((queue_rows, feat), bf16),
                pltpu.VMEM((batch_rows, feat), f32),
                pltpu.VMEM((queue_rows, feat), f32),
                pltpu.SemaphoreType.DMA((2,)),
            ],
            compiler_params=limit(56),
        )(*places, crop_image.reshape(1, batch_rows), embeddings, queue_feats)

        lines = [unit] + [shift_row(unit, z, 0) for z in range(1, z_count)]
        width = prototypes.shape[1] // row_count
        features = prototypes.shape[0]

        def strip(dy):
            places = [((other * y_count) + (y ^ dy)) * width for other in range(z_count)]
            return jnp.stack([lax.dynamic_slice(prototypes, (0, place), (features, width)) for place in places])

        strips = [shift_row(strip(dy), 0, dy) if dy else strip(dy) for dy in range(y_count)]
        lanes = [[other * y_count + own for other in range(z_count)] for own in range(y_count)]
        *lines, strips = lax.optimization_barrier((*lines, jnp.stack(strips, axis=1)))
        lines = jnp.stack(lines)
        strips = lax.all_to_all(
            strips, "row", split_axis=0, concat_axis=0, axis_index_groups=lanes, tiled=True
        )

        offsets, units = [], []
        for dy in range(y_count):
            there = shift_row(lines, 0, dy) if dy else lines
            for dx in range(x_count):
                moved = shift_proto(there, 2 * dx) if dx else there
                offsets += [(dy, 2 * dx), (dy, 2 * dx + 1)]
                units += [moved, shift_proto(moved, 1)]

        mass, sums, side, batch, columns = pl.pallas_call(
            functools.partial(make_kernel, offsets, share, total_batch),
            name="make_mass",
            out_shape=[
                jax.ShapeDtypeStruct((total_rows + feat * (1 + total_batch // width), width), bf16),
                jax.ShapeDtypeStruct((1, total_rows), f32),
                jax.ShapeDtypeStruct((1, total_batch + 128), f32),
                jax.ShapeDtypeStruct((total_batch, feat), bf16),
                jax.ShapeDtypeStruct((feat, width), bf16),
            ],
            in_specs=[SMEM, SMEM, SMEM] + [ANY] * (len(units) + 1),
            out_specs=[ANY, VMEM, VMEM, VMEM, VMEM],
            scratch_shapes=[
                pltpu.VMEM((total_rows, width), bf16),
                pltpu.VMEM((total_queue, feat), bf16),
                pltpu.VMEM((8, width), f32),
                pltpu.SemaphoreType.DMA((len(units), z_count, 2)),
                pltpu.SemaphoreType.DMA((z_count, y_count)),
                pltpu.SemaphoreType.DMA((1 + total_batch // feat,)),
                pltpu.SemaphoreType.DMA,
            ],
            compiler_params=limit(53),
        )(*places, fill_count, *units, strips)

        vectors = [pltpu.VMEM((8, total_rows), bf16), pltpu.VMEM((8, width), f32), pltpu.VMEM((8, width), f32)]
        sums = pl.pallas_call(
            functools.partial(sweep_kernel, total_batch),
            name="sweep",
            out_shape=jax.ShapeDtypeStruct((1, total_rows), f32),
            in_specs=[SMEM, ANY] + [VMEM] * z_count,
            out_specs=VMEM,
            scratch_shapes=[pltpu.VMEM((total_rows, width), bf16)]
            + vectors
            + [
                pltpu.VMEM((total_batch, feat), bf16),
                pltpu.VMEM((feat, width), bf16),
                pltpu.SemaphoreType.DMA((total_queue // BLOCK,)),
                pltpu.SemaphoreType.DMA((1 + total_batch // feat,)),
            ],
            compiler_params=limit(33),
        )(fill_count, mass, *all_sum_parts(sums))

        code_sums, column = pl.pallas_call(
            functools.partial(last_kernel, total_batch),
            name="last_sweep",
            out_shape=[
                jax.ShapeDtypeStruct((1, 2 * total_batch + 128), f32),
                jax.ShapeDtypeStruct((1, width), f32),
            ],
            in_specs=[SMEM] + [VMEM] * (2 + z_count),
            out_specs=[VMEM, VMEM],
            scratch_shapes=vectors,
            compiler_params=limit(8),
        )(fill_count, side, mass, *all_sum_parts(sums))

        code_parts = all_sum_parts(code_sums)

        def slopes(first, last, batch):
            return pl.pallas_call(
                functools.partial(slope_kernel, CROPS, first, last),
                name="slopes",
                out_shape=[
                    jax.ShapeDtypeStruct((total_batch, feat), f32),
                    jax.ShapeDtypeStruct((feat, last - first), f32),
                    jax.ShapeDtypeStruct((8, 128), f32),
                    jax.ShapeDtypeStruct((8, 128), f32),
                ],
                in_specs=[VMEM] * (3 + z_count),
                out_specs=[ANY, VMEM, VMEM, VMEM],
                scratch_shapes=[
                    pltpu.VMEM((total_batch, feat), f32),
                    pltpu.SemaphoreType.DMA((total_batch // ROWS,)),
                ],
                compiler_params=limit(24),
            )(batch, columns, column, *code_parts)

        def as_blocks(grad_columns):
            return grad_columns.astype(f16).reshape(row_count, feat // row_count, -1)

        def exchange(blocks):
            return lax.all_to_all(blocks, "row", split_axis=0, concat_axis=0, tiled=True)

        normed_part, grad_columns, loss, back = slopes(0, width, batch)
        size = half // x_count

        pieces = normed_part.reshape(z_count, y_count, 2, x_count, size, feat)

        away = shift_proto(pick(pieces, 1 - core, 2).astype(f16), 1)
        kept = pick(pieces, core, 2) + away.astype(f32)
        total = None
        for dy in range(y_count):
            for dx in range(x_count):
                part = pick(pick(kept, x ^ dx, 2), y ^ dy, 1)
                if dx or dy:
                    part = shift_xy(part.astype(f16), dx, dy).astype(f32)
                total = part if total is None else total + part
        arriving = [shift_row(pick(total, z ^ dz, 0).astype(f16), dz, 0) for dz in range(1, z_count)]

        sent = jnp.concatenate([as_blocks(grad_columns), jnp.broadcast_to(loss[0:1].astype(f16), (row_count, feat // row_count, 128))], axis=2)
        got = exchange(sent)
        grad_proto = got[:, :, :width].astype(f32)
        grad_proto = grad_proto.transpose(1, 0, 2).reshape(feat // row_count, row_count * width)
        code = got[:, 0, width:].astype(f32)
        losses = jnp.sum((code[:, 1] + code[:, 2] / 2048.0) * jnp.exp2(code[:, 0])) / total_batch
        *arriving, losses = lax.optimization_barrier((*arriving, losses))
        piece = functools.reduce(jnp.add, [part.astype(f32) for part in arriving], pick(total, z, 0))
        piece = jnp.concatenate([piece, jnp.full((8, feat), losses, f32)], axis=0)

        gathered = [piece] + [shift_proto(piece, k) for k in range(1, proto_count)]
        grad_embed, loss = pl.pallas_call(
            functools.partial(finish_kernel, proto_count),
            name="finish",
            out_shape=[
                jax.ShapeDtypeStruct((batch_rows, feat), f32),
                jax.ShapeDtypeStruct((1,), f32),
            ],
            in_specs=[SMEM] + [VMEM] * (3 + proto_count),
            out_specs=[VMEM, SMEM],
            scratch_shapes=[pltpu.VMEM((batch_rows, feat), f32)],
            compiler_params=limit(8),
        )(proto.reshape(1).astype(jnp.int32), embeddings, order, back, *gathered)
        return grad_embed, grad_proto, loss

    placed = (P("row", None), P("row", None), P("row", "proto"), P("row"), P())
    return jax.shard_map(
        body,
        mesh=mesh,
        in_specs=placed,
        out_specs=(P("row", None), P("row", "proto"), P()),
        check_vma=False,
    )
```

```python
import functools

import jax
import jax.numpy as jnp
from jax import lax
from jax.experimental import pallas as pl
from jax.experimental.pallas import tpu as pltpu
from jax.sharding import PartitionSpec as P

CROPS = 8
LOG2E = 1.4426950408889634
SOFT_SCALE = 10.0 * LOG2E
BLOCK = 1024
WIDE = 256
ROWS = 1024

f32 = jnp.float32
bf16 = jnp.bfloat16
f16 = jnp.float16

VMEM = pl.BlockSpec(memory_space=pltpu.VMEM)
SMEM = pl.BlockSpec(memory_space=pltpu.SMEM)
ANY = pl.BlockSpec(memory_space=pl.ANY)


def limit(mib):
    return pltpu.CompilerParams(vmem_limit_bytes=mib << 20)


def bf16_terms(values):
    high = values.astype(bf16)
    rest = values - high.astype(f32)
    middle = rest.astype(bf16)
    return high, middle, (rest - middle.astype(f32)).astype(bf16)


def term_rows(values):
    high, middle, low = bf16_terms(values)
    return jnp.concatenate([high, middle, low] + [jnp.zeros_like(high)] * 5, axis=0)


def sum_terms(products):
    return products[0:1] + products[1:2] + products[2:3]


def dot_nt(left, right):
    return lax.dot_general(left, right, (((1,), (1,)), ((), ())), preferred_element_type=f32)


def dot_tn(left, right):
    return lax.dot_general(left, right, (((0,), (0,)), ((), ())), preferred_element_type=f32)


def unit_rows(raw):
    values = raw.astype(f32)
    inverse = lax.rsqrt(jnp.sum(values * values, axis=1, keepdims=True) + 1e-06)
    return values * inverse, inverse


def prep_kernel(
    row_ref, proto_ref, image_ref, embed_in, queue_in, unit_ref, order_ref, embed_ref, queue_ref, sorted_ref, queued_ref, sems
):
    fetch = [
        pltpu.make_async_copy(embed_in, embed_ref, sems.at[0]),
        pltpu.make_async_copy(queue_in, queue_ref, sems.at[1]),
    ]
    for copy in fetch:
        copy.start()
    row, proto = row_ref[0], proto_ref[0]
    rows = embed_ref.shape[0]
    half = rows // 2
    images = half // CROPS
    local = image_ref[...] - row * (rows // CROPS)
    across = jnp.broadcast_to(local, (rows, rows)).astype(f32)
    down = jnp.transpose(across, (1, 0))
    first = lax.broadcasted_iota(jnp.int32, (rows, rows), 0)
    second = lax.broadcasted_iota(jnp.int32, (rows, rows), 1)
    earlier = jnp.where((across == down) & (first < second), 1.0, 0.0)
    rank = jnp.sum(earlier, axis=0, keepdims=True).astype(jnp.int32)
    upper = jnp.where(local >= images, 1, 0)
    position = upper * half + rank * images + (local - upper * images)
    order = (first == position).astype(f32).astype(bf16)
    order_ref[...] = order
    for copy in fetch:
        copy.wait()
    normed = unit_rows(embed_ref[...])[0].astype(bf16)
    sorted_ref[...] = jnp.dot(order, normed, preferred_element_type=f32)
    queued_ref[...] = unit_rows(queue_ref[...])[0]
    share = rows * unit_ref.shape[0] // (rows + queue_ref.shape[0])
    queue_share = unit_ref.shape[0] - share
    unit_ref[0:share, :] = sorted_ref[pl.ds(pl.multiple_of(proto * share, share), share), :].astype(bf16)
    unit_ref[share:, :] = queued_ref[
        pl.ds(pl.multiple_of(proto * queue_share, queue_share), queue_share), :
    ].astype(bf16)


def row_sums(column, total_batch, fill, mass_ref, out_ref, exact=False):
    width = mass_ref.shape[1]
    step = 128
    factor = column[0:1]
    ones = jnp.ones((8, 128), bf16)

    def one(start, size):
        head = size if exact else size // 4
        out_ref[0:1, pl.ds(start, head)] = sum_terms(dot_nt(column, mass_ref[pl.ds(start, head), :]))
        for rows in range(head, size, step):
            here = pl.ds(pl.multiple_of(start + rows, step), step)
            total = None
            for low in range(0, width, 256):
                pair = mass_ref[here, low : low + 128] * factor[:, low : low + 128]
                pair += mass_ref[here, low + 128 : low + 256] * factor[:, low + 128 : low + 256]
                total = pair.astype(f32) if total is None else total + pair.astype(f32)
            high = total.astype(bf16)
            low = (total - high.astype(f32)).astype(bf16)
            out_ref[0:1, here] = (dot_nt(ones, high) + dot_nt(ones, low))[0:1]

    def queue(start, size, cut):
        one(pl.multiple_of(total_batch + start, BLOCK // 2), size)

    each_block(total_batch, fill, one, None if fill is None else queue)


def kept_places(total_rows, total_batch, feat, width):
    across = width // feat
    pieces = [
        (total_rows + feat * (1 + index // across), feat * (index % across), feat * index)
        for index in range(total_batch // feat)
    ]
    return total_rows, pieces


def each_block(total_batch, fill, crops_body, queue_body):
    def crops(index, carry):
        crops_body(pl.multiple_of(index * BLOCK, BLOCK), BLOCK)
        return carry

    def queue(index, carry):
        queue_body(pl.multiple_of(index * BLOCK, BLOCK), BLOCK, False)
        return carry

    if crops_body is not None:
        lax.fori_loop(0, total_batch // BLOCK, crops, 0)
    if queue_body is not None:
        whole = lax.div(fill, BLOCK)
        rest = fill - whole * BLOCK
        lax.fori_loop(0, whole, queue, 0)
        half = BLOCK // 2

        def tail(index, carry):
            queue_body(pl.multiple_of(whole * BLOCK + index * half, half), half, True)
            return carry

        lax.fori_loop(0, lax.div(rest + (half - 1), half), tail, 0)


def make_kernel(offsets, share, total_batch, row_ref, proto_ref, fill_ref, *refs):
    *inputs, mass_out, sums_ref, side_ref, batch_ref, columns_ref, mass_ref, queue_ref, col_ref, sems, strip_sems, kept_sems, out_sems = refs
    *units, strips_ref = inputs
    row, proto = row_ref[0], proto_ref[0]
    fill = fill_ref[0]
    z_count, unit_rows_count, _ = units[0].shape
    queue_share = unit_rows_count - share
    proto_count = 1 + max(other for _, other in offsets)
    y_count = 1 + max(y for y, _ in offsets)
    strip_copies = []
    z_count, y_count, features, _ = strips_ref.shape
    for z in range(z_count):
        for y in range(y_count):
            first = pl.multiple_of((z * y_count + (lax.rem(row, y_count) ^ y)) * features, features)
            strip_copies.append(
                pltpu.make_async_copy(
                    strips_ref.at[z, y], columns_ref.at[pl.ds(first, features), :], strip_sems.at[z, y]
                )
            )
    for copy in strip_copies:
        copy.start()
    copies = []
    for index, (unit, (y, other)) in enumerate(zip(units, offsets)):
        for z in range(z_count):
            place = (row ^ (z * y_count + y)) * proto_count + (proto ^ other)
            crops = pl.multiple_of(place * share, share)
            queued = pl.multiple_of(place * queue_share, queue_share)
            copies.append(
                pltpu.make_async_copy(
                    unit.at[z, pl.ds(0, share), :],
                    batch_ref.at[pl.ds(crops, share), :],
                    sems.at[index, z, 0],
                )
            )
            copies.append(
                pltpu.make_async_copy(
                    unit.at[z, pl.ds(share, queue_share), :],
                    queue_ref.at[pl.ds(queued, queue_share), :],
                    sems.at[index, z, 1],
                )
            )
    for copy in copies[0::2] + copies[1::2]:
        copy.start()
    total_queue = queue_ref.shape[0]
    total_rows = total_batch + total_queue
    width = columns_ref.shape[1]
    col_ref[...] = jnp.zeros_like(col_ref)
    sums_ref[...] = jnp.zeros_like(sums_ref)
    ones = jnp.ones((8, 128), bf16)
    for copy in strip_copies:
        copy.wait()
    bound = jnp.max(jnp.abs(columns_ref[...].astype(f32)))
    side_ref[0:1, total_batch:] = jnp.full((1, 128), bound, f32)
    for copy in copies[0::2]:
        copy.wait()

    def add_columns(low, mass):
        col_ref[:, low : low + WIDE] += jnp.sum(mass.reshape(mass.shape[0] // 8, 8, WIDE), axis=0)

    feat = columns_ref.shape[0]
    first, pieces = kept_places(total_rows, total_batch, feat, width)
    kept = [pltpu.make_async_copy(columns_ref, mass_out.at[pl.ds(first, feat), :], kept_sems.at[0])]
    for index, (place, lane, crop) in enumerate(pieces):
        kept.append(
            pltpu.make_async_copy(
                batch_ref.at[pl.ds(crop, feat), :],
                mass_out.at[pl.ds(place, feat), pl.ds(lane, feat)],
                kept_sems.at[1 + index],
            )
        )
    for copy in kept:
        copy.start()

    def keep(start, size):
        place = pl.ds(pl.multiple_of(start, BLOCK // 2), size)
        return pltpu.make_async_copy(mass_ref.at[place, :], mass_out.at[place, :], out_sems)

    def crops_block(start, size):
        rows = batch_ref[pl.ds(start, BLOCK), :]
        lanes = None
        for low in range(0, width, WIDE):
            scores = jnp.dot(rows, columns_ref[:, low : low + WIDE], preferred_element_type=f32)
            soft = jnp.exp2(scores * SOFT_SCALE)
            mass = soft * soft
            mass_ref[pl.ds(start, BLOCK), low : low + WIDE] = mass.astype(bf16)
            add_columns(low, mass)
            for lane in range(0, WIDE, 128):
                part = soft[:, lane : lane + 128]
                lanes = part if lanes is None else lanes + part
        high, middle, small = bf16_terms(lanes)
        total = dot_nt(ones, high) + dot_nt(ones, middle) + dot_nt(ones, small)
        side_ref[0:1, pl.ds(start, BLOCK)] = total[0:1]
        keep(start, size).start()

    each_block(total_batch, fill, crops_block, None)

    for copy in copies[1::2]:
        copy.wait()

    def queue_block(start, size, cut):
        rows = queue_ref[pl.ds(start, size), :]
        place = pl.ds(pl.multiple_of(total_batch + start, BLOCK // 2), size)
        for low in range(0, width, WIDE):
            scores = jnp.dot(rows, columns_ref[:, low : low + WIDE], preferred_element_type=f32)
            soft = jnp.exp2(scores * SOFT_SCALE)
            mass = soft * soft
            if cut:
                live = lax.broadcasted_iota(jnp.int32, (size, WIDE), 0) < fill - start
                mass = jnp.where(live, mass, 0.0)
            mass_ref[place, low : low + WIDE] = mass.astype(bf16)
            add_columns(low, mass)
        keep(total_batch + start, size).start()

    each_block(total_batch, fill, None, queue_block)
    column = term_rows(1.0 / jnp.sum(col_ref[...], axis=0, keepdims=True))
    row_sums(column, total_batch, fill, mass_ref, sums_ref)
    each_block(
        total_batch,
        fill,
        lambda start, size: keep(start, size).wait(),
        lambda start, size, cut: keep(total_batch + start, size).wait(),
    )
    for copy in kept:
        copy.wait()


def column_factor(fill, total_batch, parts, mass_ref, scale_ref, col_ref, spare_ref, settle=None, make=None, ready=None):
    total_rows = scale_ref.shape[1]
    total = parts[0][0:1, 0:total_rows]
    for part in parts[1:]:
        total = total + part[0:1, 0:total_rows]
    place = lax.broadcasted_iota(jnp.int32, (1, total_rows), 1)
    scale = jnp.where(place < total_batch + fill, 1.0 / total, 0.0)
    scale_ref[...] = term_rows(scale)
    col_ref[...] = jnp.zeros_like(col_ref)
    spare_ref[...] = jnp.zeros_like(spare_ref)

    def add(start, size):
        head = 3 * size // 4
        rows, rest = pl.ds(start, head), pl.ds(pl.multiple_of(start + head, 128), size - head)
        col_ref[...] += jnp.dot(scale_ref[:, rows], mass_ref[rows, :], preferred_element_type=f32)
        high, middle, low = (scale_ref[i : i + 1, rest].astype(f32) for i in range(3))
        factor = jnp.transpose(jnp.broadcast_to(high + middle + low, (128, size - head)), (1, 0))
        for low in range(0, mass_ref.shape[1], 128):
            part = mass_ref[rest, low : low + 128].astype(f32) * factor
            spare_ref[:, low : low + 128] += jnp.sum(part.reshape((size - head) // 8, 8, 128), axis=0)

    def crops(start, size):
        if make is not None:
            make(start, size)
        add(start, size)

    def queue(start, size, cut):
        if ready is not None:
            ready(start, size)
        add(pl.multiple_of(total_batch + start, BLOCK // 2), size)

    if settle is not None:
        settle()
    each_block(total_batch, fill, crops, queue)
    return 1.0 / (sum_terms(col_ref[...]) + jnp.sum(spare_ref[...], axis=0, keepdims=True))


def sweep_kernel(total_batch, fill_ref, mass_in, *refs):
    *parts, sums_ref, mass_ref, scale_ref, col_ref, spare_ref, batch_ref, columns_ref, sems, kept_sems = refs
    fill = fill_ref[0]
    feat, width = columns_ref.shape
    first, pieces = kept_places(mass_ref.shape[0], total_batch, feat, width)
    kept = [pltpu.make_async_copy(mass_in.at[pl.ds(first, feat), :], columns_ref, kept_sems.at[0])]
    for index, (place, lane, crop) in enumerate(pieces):
        kept.append(
            pltpu.make_async_copy(
                mass_in.at[pl.ds(place, feat), pl.ds(lane, feat)],
                batch_ref.at[pl.ds(crop, feat), :],
                kept_sems.at[1 + index],
            )
        )
    for copy in kept:
        copy.start()

    def fetch(start, size):
        rows = pl.ds(pl.multiple_of(total_batch + start, BLOCK // 2), size)
        return pltpu.make_async_copy(mass_in.at[rows, :], mass_ref.at[rows, :], sems.at[lax.div(start, BLOCK // 2)])

    each_block(total_batch, fill, None, lambda start, size, cut: fetch(start, size).start())

    def settle():
        for copy in kept:
            copy.wait()

    def make(start, size):
        rows = pl.ds(start, size)
        crops = batch_ref[rows, :]
        for low in range(0, width, WIDE):
            scores = jnp.dot(crops, columns_ref[:, low : low + WIDE], preferred_element_type=f32)
            soft = jnp.exp2(scores * SOFT_SCALE)
            mass_ref[rows, low : low + WIDE] = (soft * soft).astype(bf16)

    column = column_factor(
        fill,
        total_batch,
        parts,
        mass_ref,
        scale_ref,
        col_ref,
        spare_ref,
        settle,
        make,
        lambda start, size: fetch(start, size).wait(),
    )
    sums_ref[...] = jnp.zeros_like(sums_ref)
    row_sums(term_rows(column), total_batch, fill, mass_ref, sums_ref)


def last_kernel(total_batch, fill_ref, side_ref, mass_ref, *refs):
    *parts, sums_ref, column_ref, scale_ref, col_ref, spare_ref = refs
    fill = fill_ref[0]
    column = column_factor(fill, total_batch, parts, mass_ref, scale_ref, col_ref, spare_ref)
    column_ref[...] = column
    sums_ref[0:1, total_batch:] = side_ref[...]
    row_sums(term_rows(column), total_batch, None, mass_ref, sums_ref, True)


def slope_kernel(crop_count, first, last, batch_ref, columns_ref, column_ref, *refs):
    *parts, normed_out, grad_ref, loss_ref, back_ref, normed_ref, sems = refs
    total_batch, width = batch_ref.shape[0], last - first
    rows = ROWS
    wide = min(width, WIDE)
    grad_ref[...] = jnp.zeros_like(grad_ref)
    loss_ref[...] = jnp.zeros_like(loss_ref)

    bound = functools.reduce(jnp.add, [part[0:1, 2 * total_batch :] for part in parts])
    bound = 20.0 * bound + 1e-30
    back_ref[...] = jnp.broadcast_to(bound / 32768.0, (8, 128))
    scale = jnp.concatenate([32768.0 / bound] * (batch_ref.shape[1] // 128), axis=1)

    def keep(index):
        place = pl.ds(pl.multiple_of(index * rows, rows), rows)
        return pltpu.make_async_copy(normed_ref.at[place, :], normed_out.at[place, :], sems.at[index])

    def one(index, carry):
        start = pl.multiple_of(index * rows, rows)
        here = pl.ds(start, rows)

        later = pl.ds(pl.multiple_of(total_batch + start, rows), rows)
        code, soft_line = parts[0][0:1, here], parts[0][0:1, later]
        for part in parts[1:]:
            code, soft_line = code + part[0:1, here], soft_line + part[0:1, later]
        lines = [1.0 / ((crop_count - 1) * code), 10.0 / soft_line, jnp.log(soft_line)]
        factors = jnp.transpose(jnp.concatenate(lines + [jnp.zeros((125, rows), f32)], axis=0), (1, 0))
        code_factor, soft_factor, log_soft = (factors[:, i : i + 1] for i in range(3))
        crops = batch_ref[here, :]
        crops_t = jnp.transpose(crops.astype(f32), (1, 0)).astype(bf16)
        normed = jnp.zeros((rows, crops.shape[1]), f32)
        loss = jnp.zeros((8, 128), f32)
        for low in range(0, width, wide):
            place = slice(first + low, first + low + wide)
            columns = columns_ref[:, place]
            scores = jnp.dot(crops, columns, preferred_element_type=f32)
            soft = jnp.exp2(scores * SOFT_SCALE)
            assigned = (soft * soft) * column_ref[0:1, place] * code_factor
            slabs = assigned.reshape(rows // 128, crop_count, 128 // crop_count, wide)
            grouped = jnp.sum(slabs, axis=1, keepdims=True)
            targets = (grouped - slabs).reshape(rows, wide)
            logits = (soft * soft_factor - targets * 10.0).astype(bf16)
            terms = targets * (log_soft - scores * 10.0)
            folded = jnp.sum(terms.reshape(rows // 8, 8, wide), axis=0)
            for lane in range(0, wide, 128):
                loss = loss + folded[:, lane : lane + 128]
            grad_ref[:, low : low + wide] += jnp.dot(crops_t, logits, preferred_element_type=f32)
            normed = normed + dot_nt(logits, columns)
        normed_ref[here, :] = normed * scale
        keep(index).start()
        loss_ref[...] += loss
        return carry

    lax.fori_loop(0, total_batch // rows, one, 0)

    loss = jnp.maximum(jnp.sum(loss_ref[...]), 1e-30)
    exponent = jnp.floor(jnp.log2(jnp.full((1, 128), loss, f32)))
    mantissa = loss / jnp.exp2(exponent)
    high = jnp.floor(mantissa * 1024.0) / 1024.0
    lane = lax.broadcasted_iota(jnp.int32, (1, 128), 1)
    loss_ref[...] = jnp.broadcast_to(
        jnp.where(lane == 0, exponent, jnp.where(lane == 1, high, (mantissa - high) * 2048.0)), (8, 128)
    )

    def kept(index, carry):
        keep(index).wait()
        return carry

    lax.fori_loop(0, total_batch // rows, kept, 0)


def finish_kernel(piece_count, proto_ref, embed_ref, order_ref, back_ref, *refs):
    *pieces, out_ref, loss_ref, sorted_ref = refs
    rows = embed_ref.shape[0]
    size = rows // piece_count
    proto = proto_ref[0]
    for index, piece in enumerate(pieces):
        other = proto ^ index
        place = (other % 2) * (piece_count // 2) + other // 2
        sorted_ref[pl.ds(pl.multiple_of(place * size, size), size), :] = piece[0:size, :]
    loss_ref[0] = jnp.max(functools.reduce(jnp.add, [piece[size:, 0:128] for piece in pieces]))
    order = order_ref[...]
    high, middle, low = bf16_terms(sorted_ref[...])
    grad = dot_tn(order, high) + dot_tn(order, middle) + dot_tn(order, low)
    grad = grad * back_ref[0:1, 0:1]
    exact, inverse = unit_rows(embed_ref[...])
    out_ref[...] = inverse * (grad - exact * jnp.sum(exact * grad, axis=1, keepdims=True))


def solution(mesh):
    row_count, proto_count = mesh.shape["row"], mesh.shape["proto"]
    z_count = min(4, row_count)
    y_count = row_count // z_count
    x_count = proto_count // 2

    def shift_row(values, z, y):
        offset = z * y_count + y
        return lax.ppermute(values, "row", [(i, i ^ offset) for i in range(row_count)])

    def shift_proto(values, offset):
        return lax.ppermute(values, "proto", [(i, i ^ offset) for i in range(proto_count)])

    def shift_xy(values, x, y):
        pairs = []
        for i in range(row_count):
            for j in range(proto_count):
                pairs.append((i * proto_count + j, (i ^ y) * proto_count + (j ^ (2 * x))))
        return lax.ppermute(values, ("row", "proto"), pairs)

    def all_sum_parts(values):
        values = values + shift_proto(values, 1)
        moved = [shift_xy(values, x, y) for y in range(y_count) for x in range(x_count) if x or y]
        values = functools.reduce(jnp.add, moved, values)
        return [values] + [shift_row(values, z, 0) for z in range(1, z_count)]

    def body(embeddings, queue_feats, prototypes, crop_image, fill_count):
        batch_rows, feat = embeddings.shape
        queue_rows = queue_feats.shape[0]
        share, queue_share = batch_rows // proto_count, queue_rows // proto_count
        half = batch_rows // 2
        total_batch, total_queue = batch_rows * row_count, queue_rows * row_count
        total_rows = total_batch + total_queue
        row, proto = lax.axis_index("row"), lax.axis_index("proto")
        core, x, y, z = proto % 2, proto // 2, row % y_count, row // y_count
        places = [row.reshape(1).astype(jnp.int32), proto.reshape(1).astype(jnp.int32)]
        unit_rows_count = share + queue_share

        def pick(values, index, axis):
            return lax.dynamic_index_in_dim(values, index, axis, keepdims=False)

        unit, order = pl.pallas_call(
            prep_kernel,
            name="prep",
            out_shape=[
                jax.ShapeDtypeStruct((unit_rows_count, feat), bf16),
                jax.ShapeDtypeStruct((batch_rows, batch_rows), bf16),
            ],
            in_specs=[SMEM, SMEM, VMEM, ANY, ANY],
            out_specs=[VMEM, VMEM],
            scratch_shapes=[
                pltpu.VMEM((batch_rows, feat), bf16),
                pltpu.VMEM((queue_rows, feat), bf16),
                pltpu.VMEM((batch_rows, feat), f32),
                pltpu.VMEM((queue_rows, feat), f32),
                pltpu.SemaphoreType.DMA((2,)),
            ],
            compiler_params=limit(56),
        )(*places, crop_image.reshape(1, batch_rows), embeddings, queue_feats)

        lines = [unit] + [shift_row(unit, z, 0) for z in range(1, z_count)]
        width = prototypes.shape[1] // row_count
        features = prototypes.shape[0]

        def strip(dy):
            places = [((other * y_count) + (y ^ dy)) * width for other in range(z_count)]
            return jnp.stack([lax.dynamic_slice(prototypes, (0, place), (features, width)) for place in places])

        strips = [shift_row(strip(dy), 0, dy) if dy else strip(dy) for dy in range(y_count)]
        lanes = [[other * y_count + own for other in range(z_count)] for own in range(y_count)]
        *lines, strips = lax.optimization_barrier((*lines, jnp.stack(strips, axis=1)))
        lines = jnp.stack(lines)
        strips = lax.all_to_all(
            strips, "row", split_axis=0, concat_axis=0, axis_index_groups=lanes, tiled=True
        )

        offsets, units = [], []
        for dy in range(y_count):
            there = shift_row(lines, 0, dy) if dy else lines
            for dx in range(x_count):
                moved = shift_proto(there, 2 * dx) if dx else there
                offsets += [(dy, 2 * dx), (dy, 2 * dx + 1)]
                units += [moved, shift_proto(moved, 1)]

        mass, sums, side, batch, columns = pl.pallas_call(
            functools.partial(make_kernel, offsets, share, total_batch),
            name="make_mass",
            out_shape=[
                jax.ShapeDtypeStruct((total_rows + feat * (1 + total_batch // width), width), bf16),
                jax.ShapeDtypeStruct((1, total_rows), f32),
                jax.ShapeDtypeStruct((1, total_batch + 128), f32),
                jax.ShapeDtypeStruct((total_batch, feat), bf16),
                jax.ShapeDtypeStruct((feat, width), bf16),
            ],
            in_specs=[SMEM, SMEM, SMEM] + [ANY] * (len(units) + 1),
            out_specs=[ANY, VMEM, VMEM, VMEM, VMEM],
            scratch_shapes=[
                pltpu.VMEM((total_rows, width), bf16),
                pltpu.VMEM((total_queue, feat), bf16),
                pltpu.VMEM((8, width), f32),
                pltpu.SemaphoreType.DMA((len(units), z_count, 2)),
                pltpu.SemaphoreType.DMA((z_count, y_count)),
                pltpu.SemaphoreType.DMA((1 + total_batch // feat,)),
                pltpu.SemaphoreType.DMA,
            ],
            compiler_params=limit(53),
        )(*places, fill_count, *units, strips)

        vectors = [pltpu.VMEM((8, total_rows), bf16), pltpu.VMEM((8, width), f32), pltpu.VMEM((8, width), f32)]
        sums = pl.pallas_call(
            functools.partial(sweep_kernel, total_batch),
            name="sweep",
            out_shape=jax.ShapeDtypeStruct((1, total_rows), f32),
            in_specs=[SMEM, ANY] + [VMEM] * z_count,
            out_specs=VMEM,
            scratch_shapes=[pltpu.VMEM((total_rows, width), bf16)]
            + vectors
            + [
                pltpu.VMEM((total_batch, feat), bf16),
                pltpu.VMEM((feat, width), bf16),
                pltpu.SemaphoreType.DMA((total_queue // (BLOCK // 2),)),
                pltpu.SemaphoreType.DMA((1 + total_batch // feat,)),
            ],
            compiler_params=limit(33),
        )(fill_count, mass, *all_sum_parts(sums))

        code_sums, column = pl.pallas_call(
            functools.partial(last_kernel, total_batch),
            name="last_sweep",
            out_shape=[
                jax.ShapeDtypeStruct((1, 2 * total_batch + 128), f32),
                jax.ShapeDtypeStruct((1, width), f32),
            ],
            in_specs=[SMEM] + [VMEM] * (2 + z_count),
            out_specs=[VMEM, VMEM],
            scratch_shapes=vectors,
            compiler_params=limit(8),
        )(fill_count, side, mass, *all_sum_parts(sums))

        code_parts = all_sum_parts(code_sums)

        def slopes(first, last, batch):
            return pl.pallas_call(
                functools.partial(slope_kernel, CROPS, first, last),
                name="slopes",
                out_shape=[
                    jax.ShapeDtypeStruct((total_batch, feat), f32),
                    jax.ShapeDtypeStruct((feat, last - first), f32),
                    jax.ShapeDtypeStruct((8, 128), f32),
                    jax.ShapeDtypeStruct((8, 128), f32),
                ],
                in_specs=[VMEM] * (3 + z_count),
                out_specs=[ANY, VMEM, VMEM, VMEM],
                scratch_shapes=[
                    pltpu.VMEM((total_batch, feat), f32),
                    pltpu.SemaphoreType.DMA((total_batch // ROWS,)),
                ],
                compiler_params=limit(24),
            )(batch, columns, column, *code_parts)

        def as_blocks(grad_columns):
            return grad_columns.astype(f16).reshape(row_count, feat // row_count, -1)

        def exchange(blocks):
            return lax.all_to_all(blocks, "row", split_axis=0, concat_axis=0, tiled=True)

        normed_part, grad_columns, loss, back = slopes(0, width, batch)
        size = half // x_count

        pieces = normed_part.reshape(z_count, y_count, 2, x_count, size, feat)

        away = shift_proto(pick(pieces, 1 - core, 2).astype(f16), 1)
        kept = pick(pieces, core, 2) + away.astype(f32)
        total = None
        for dy in range(y_count):
            for dx in range(x_count):
                part = pick(pick(kept, x ^ dx, 2), y ^ dy, 1)
                if dx or dy:
                    part = shift_xy(part.astype(f16), dx, dy).astype(f32)
                total = part if total is None else total + part
        arriving = [shift_row(pick(total, z ^ dz, 0).astype(f16), dz, 0) for dz in range(1, z_count)]

        sent = jnp.concatenate([as_blocks(grad_columns), jnp.broadcast_to(loss[0:1].astype(f16), (row_count, feat // row_count, 128))], axis=2)
        got = exchange(sent)
        grad_proto = got[:, :, :width].astype(f32)
        grad_proto = grad_proto.transpose(1, 0, 2).reshape(feat // row_count, row_count * width)
        code = got[:, 0, width:].astype(f32)
        losses = jnp.sum((code[:, 1] + code[:, 2] / 2048.0) * jnp.exp2(code[:, 0])) / total_batch
        *arriving, losses = lax.optimization_barrier((*arriving, losses))
        piece = functools.reduce(jnp.add, [part.astype(f32) for part in arriving], pick(total, z, 0))
        piece = jnp.concatenate([piece, jnp.full((8, feat), losses, f32)], axis=0)

        gathered = [piece] + [shift_proto(piece, k) for k in range(1, proto_count)]
        grad_embed, loss = pl.pallas_call(
            functools.partial(finish_kernel, proto_count),
            name="finish",
            out_shape=[
                jax.ShapeDtypeStruct((batch_rows, feat), f32),
                jax.ShapeDtypeStruct((1,), f32),
            ],
            in_specs=[SMEM] + [VMEM] * (3 + proto_count),
            out_specs=[VMEM, SMEM],
            scratch_shapes=[pltpu.VMEM((batch_rows, feat), f32)],
            compiler_params=limit(8),
        )(proto.reshape(1).astype(jnp.int32), embeddings, order, back, *gathered)
        return grad_embed, grad_proto, loss

    placed = (P("row", None), P("row", None), P("row", "proto"), P("row"), P())
    return jax.shard_map(
        body,
        mesh=mesh,
        in_specs=placed,
        out_specs=(P("row", None), P("row", "proto"), P()),
        check_vma=False,
    )
```
